512 devices in a mesh: gx: 16 (over x, z_hi), gy: 32 (over y, z_lo, core).
Axes of the slice: x: 4, y: 4, z: 16 (z_hi: 4, z_lo: 4; z = z_hi * 4 + z_lo), core: 2. Of those that a mesh axis runs over, the one named last changes fastest.
Arguments:
- nest_wind: float32 [16, 1536, 6144], P(None, 'gy', 'gx'), may hold values from -6 to 6
- parent_wind: float32 [16, 512, 2048], P(None, 'gy', 'gx'), may hold values from -6 to 6
- diffusion: float32 [16], replicated, may hold values from 0.02 to 0.1
- drift: float32 [2, 16], replicated, may hold values from 0.05 to 0.3
- disk_sites: int32 [2, 32, 16, 8], P(None, 'gy', 'gx'), may hold values from 0 to 383, as said below
- disk_live: int32 [32, 16, 8], P('gy', 'gx'), may hold values from 0 to 1, as said below
- disk_coef: float32 [32, 16, 8], P('gy', 'gx'), may hold values from 0.05 to 0.3
Outputs:
- nest_out: float32 [16, 1536, 6144], P(None, 'gy', 'gx')
- parent_out: float32 [16, 512, 2048], P(None, 'gy', 'gx')
The draws below stay inside these ranges and needn't reach their ends.
Inputs may be any that keep to these rules, and one draw needn't show every extreme that they name: `disk_sites`: row within 0 to 47 and column within 0 to 383 of the owner tile. `disk_live`: the live slots of a tile come first; every tile has one or more; in some rows of tiles every tile has all 8 slots live.
All inputs are finite; a program needn't handle non-finite values.
Results may differ from the reference program's by a relative error of at most 0.00011.
Values sent between devices are 32-bit elements; how exact they have to be, the bound alone decides.
A program may use at most 128 MiB of HBM per device.

```python
import math
import jax
import jax.numpy as jnp
from jax import lax

C = 16
NYD = 48
NXD = 384
MAXD = 8
FOOT = 6
NY = 1536
NX = 6144
NPY = 512
NPX = 2048
N_GX = 16
N_GY = 32


def draw_disk_sites(key, part):
    key = jax.random.fold_in(key, 11)
    key_rows, key_cols = jax.random.split(key)
    rows = jax.random.randint(key_rows, (N_GY, N_GX, MAXD), 0, NYD)
    cols = jax.random.randint(key_cols, (N_GY, N_GX, MAXD), 0, NXD)
    rows = rows.at[0, 0, 0].set(0).at[0, 0, 1].set(NYD - 1)
    cols = cols.at[0, 0, 0].set(0).at[0, 0, 1].set(NXD - 1)
    return jnp.stack([rows, cols]).astype(jnp.int32)


def draw_disk_live(key, part):
    key = jax.random.fold_in(key, 23)
    key_shift, key_count = jax.random.split(key)
    offset = jax.random.randint(key_shift, (), 0, 4)
    farm = (jnp.arange(N_GY) + offset) % 4 == 0
    counts = jax.random.randint(key_count, (N_GY, N_GX), 1, MAXD // 2 + 1)
    counts = jnp.where(farm[:, None], MAXD, counts)
    return (jnp.arange(MAXD)[None, None, :] < counts[:, :, None]).astype(jnp.int32)


def block_scale(key, extent, pieces, smallest, largest):
    def one(axis_at, shards_of):
        draws = jax.random.uniform(jax.random.fold_in(jax.random.fold_in(key, 6), axis_at), (shards_of,), jnp.float32, smallest / len(pieces), largest / len(pieces))
        return jnp.repeat(jnp.exp(draws), extent[axis_at] // shards_of).reshape((-1,) + (1,) * (len(extent) - axis_at - 1))

    loudness = one(*pieces[0])
    for cut in pieces[1:]:
        loudness = loudness * one(*cut)
    return loudness


def gaussian(stream_key, shape, scale, reach, cuts=(), kind=jnp.bfloat16):
    gain = block_scale(stream_key, shape, cuts, -0.22, 0.18) if cuts else 1.0
    values = jax.random.normal(stream_key, shape, jnp.float32) * scale * gain
    return jnp.minimum(jnp.maximum(values, -reach), reach).astype(kind)


def setup_inputs(seed: int = 0) -> dict:
    streams_of = jax.random.split(jax.random.key(seed), 8)
    return {
        "nest_wind": gaussian(streams_of[0], (C, NY, NX), 1.0, 6.0, ((1, 32), (2, 16)), jnp.float32),
        "parent_wind": gaussian(streams_of[1], (C, NPY, NPX), 1.0, 6.0, ((1, 32), (2, 16)), jnp.float32),
        "diffusion": jnp.clip(jax.random.uniform(streams_of[2], (C,), jnp.float32, 0.02, 0.1), 0.02, 0.1),
        "drift": jnp.clip(jax.random.uniform(streams_of[3], (2, C), jnp.float32, 0.05, 0.3), 0.05, 0.3),
        "disk_sites": draw_disk_sites(jax.random.fold_in(streams_of[7], 71), 0),
        "disk_live": draw_disk_live(jax.random.fold_in(streams_of[7], 71), 0),
        "disk_coef": jnp.clip(jnp.exp(math.log(0.3) - 1.7917595 * jax.random.uniform(streams_of[6], (N_GY, N_GX, MAXD), jnp.float32) ** block_scale(streams_of[6], (N_GY, N_GX, MAXD), ((0, 32), (1, 16)), -0.2, 0.2)), 0.05, 0.3),
    }


SIGMA = 2.0
HIGH = lax.Precision.HIGHEST

def advance(padded, diffuse, drift):
    centre = padded[:, 1:-1, 1:-1]
    west = padded[:, 1:-1, :-2]
    east = padded[:, 1:-1, 2:]
    south = padded[:, :-2, 1:-1]
    north = padded[:, 2:, 1:-1]
    spread = east + west + north + south - 4.0 * centre
    return centre + diffuse[:, None, None] * spread - drift[0][:, None, None] * (centre - west) - drift[1][:, None, None] * (centre - south)

def padone(field):
    return jnp.pad(field, ((0, 0), (1, 1), (1, 1)))

def weights(count):
    cells = jnp.arange(count, dtype=jnp.int32)
    coarse = cells // 3
    rest = cells % 3
    slots = jnp.arange(count // 3 + 2, dtype=jnp.int32)
    lower = jnp.where(rest == 0, 1.0 / 3.0, 0.0)
    middle = jnp.where(rest == 1, 1.0, 2.0 / 3.0)
    upper = jnp.where(rest == 2, 1.0 / 3.0, 0.0)
    table = lower[:, None] * (slots[None, :] == coarse[:, None]) + middle[:, None] * (slots[None, :] == coarse[:, None] + 1) + upper[:, None] * (slots[None, :] == coarse[:, None] + 2)
    return table.astype(jnp.float32)

def interpolate(padded, row_table, col_table):
    first = jnp.einsum('cmn,xn->cmx', padded, col_table, precision=HIGH)
    return jnp.einsum('ym,cmx->cyx', row_table, first, precision=HIGH)

def footprint(offset):
    return jnp.exp(-(offset * offset) / (2.0 * SIGMA * SIGMA))

def thrust(nest, rows, cols, live, coef):
    levels = nest.shape[0] // 2
    east_part = nest[:levels, rows, cols]
    north_part = nest[levels:, rows, cols]
    speed = jnp.sqrt(east_part * east_part + north_part * north_part + 1.0)
    scale = -(coef * live)
    return jnp.concatenate([scale * east_part * speed, scale * north_part * speed], axis=0)

def smooth(padded):
    across = (padded[:, :, :-2] + 2.0 * padded[:, :, 1:-1] + padded[:, :, 2:]) * 0.25
    return (across[:, :-2] + 2.0 * across[:, 1:-1] + across[:, 2:]) * 0.25

def reference(nest_wind, parent_wind, diffusion, drift, disk_sites, disk_live, disk_coef):
    rows = (disk_sites[0] + (jnp.arange(N_GY, dtype=jnp.int32) * NYD)[:, None, None]).reshape(-1)
    cols = (disk_sites[1] + (jnp.arange(N_GX, dtype=jnp.int32) * NXD)[None, :, None]).reshape(-1)
    live = disk_live.reshape(-1).astype(jnp.float32)
    coef = disk_coef.reshape(-1)
    parent_new = advance(padone(parent_wind), diffusion / 3.0, drift)
    row_table = weights(NY)
    col_table = weights(NX)
    bound_old = interpolate(padone(parent_wind), row_table, col_table)
    bound_new = interpolate(padone(parent_new), row_table, col_table)
    row_ids = jnp.arange(NY, dtype=jnp.int32)
    col_ids = jnp.arange(NX, dtype=jnp.int32)
    cycle = ((row_ids == 0) | (row_ids == NY - 1))[:, None] | ((col_ids == 0) | (col_ids == NX - 1))[None, :]
    offsets = jnp.arange(-FOOT, FOOT + 1, dtype=jnp.int32)
    profile = footprint(offsets.astype(jnp.float32))
    row_index = rows[:, None, None] + FOOT + offsets[None, :, None]
    col_index = cols[:, None, None] + FOOT + offsets[None, None, :]
    nest = nest_wind
    for step in range(1, 4):
        amounts = thrust(nest, rows, cols, live, coef)
        values = amounts[:, :, None, None] * profile[None, None, :, None] * profile[None, None, None, :]
        canvas = jnp.zeros((C, NY + 2 * FOOT, NX + 2 * FOOT), jnp.float32)
        canvas = canvas.at[:, row_index, col_index].add(values)
        force = canvas[:, FOOT:FOOT + NY, FOOT:FOOT + NX]
        stepped = advance(padone(nest), diffusion, drift) + force
        bound = bound_old + step / 3.0 * (bound_new - bound_old)
        nest = jnp.where(cycle[None], bound, stepped)
    average = nest.reshape(C, NPY, 3, NPX, 3).mean(axis=(2, 4))
    mixed = parent_new + 0.5 * (average - parent_new)
    return (nest, smooth(padone(mixed)))
```

```python
import functools

import jax
import jax.numpy as jnp
from jax import lax
from jax.experimental import pallas as pl
from jax.experimental.pallas import tpu as pltpu
from jax.sharding import PartitionSpec as P

C = 16
NYD = 48
NXD = 384
PYD = 16
PXD = 128
MAXD = 8
FOOT = 6
H = 16
PH = 8
ROWS = NYD + 2 * H
PROWS = PYD + 2 * PH
WIDE = 512
PWIDE = 256
SLOT = 80
CHUNK = 6
F32 = jnp.float32
BF16 = jnp.bfloat16
MESH = pl.DeviceIdType.MESH
AROUND = ((0, 0), (0, -1), (0, 1), (-1, 0), (1, 0), (-1, -1), (1, -1), (-1, 1), (1, 1))


def lanes_of(shape):
    return lax.broadcasted_iota(jnp.int32, shape, len(shape) - 1)


def turn(value, shift):
    shift = shift % value.shape[-1] if isinstance(shift, int) else shift
    if isinstance(shift, int) and shift == 0:
        return value
    return pltpu.roll(value, shift, value.ndim - 1)


def thrusts(wind, scale):
    half = C // 2
    east, north = wind[:half], wind[half:]
    speed = jnp.sqrt(east * east + north * north + 1.0)
    return scale * wind * jnp.concatenate([speed, speed], axis=0)


def exchange(tiles_x, tiles_y, nest, parent, sites, live, coef,
             own, south, north, pown, psouth, pnorth, west, east, corner, info,
             pack_w, pack_e, in_sem, send_sem, recv_sem):
    gx, gy = lax.axis_index("gx"), lax.axis_index("gy")

    def device(dx, dy):
        return (lax.rem(gx + dx + tiles_x, tiles_x), lax.rem(gy + dy + tiles_y, tiles_y))

    barrier = pltpu.get_barrier_semaphore()
    for dx, dy in AROUND[1:]:
        pl.semaphore_signal(barrier, inc=1, device_id=device(dx, dy), device_id_type=MESH)

    loads = [pltpu.make_async_copy(nest.at[c], own.at[:, c, :], in_sem.at[c]) for c in range(C)]
    loads += [pltpu.make_async_copy(parent.at[c], pown.at[:, c, :], in_sem.at[C + c]) for c in range(C)]
    for load in loads:
        load.start()
    for load in loads:
        load.wait()

    lane = lanes_of((C, PXD))
    wide_lane = lanes_of((C, NXD))
    wind = jnp.zeros((C, PXD), F32)
    scale = jnp.zeros((C, PXD), F32)
    spot = jnp.zeros((C, PXD), F32)
    for s in range(MAXD):
        row, col = sites[0, 0, 0, s], sites[1, 0, 0, s]
        line = own[row]
        value = jnp.sum(jnp.where(wide_lane == col, line, 0.0), axis=1, keepdims=True)
        wind = jnp.where(lane == s, value, wind)
        push = -(coef[0, 0, s] * live[0, 0, s].astype(F32))
        scale = jnp.where(lane == s, push, scale)
        spot = jnp.where(lane == MAXD + s, row.astype(F32), spot)
        spot = jnp.where(lane == 2 * MAXD + s, col.astype(F32), spot)
        spot = jnp.where(lane == 3 * MAXD + s, push, spot)
    mine = thrusts(wind, scale) + spot
    info[0] = mine

    for pack, tile, first in ((pack_w, 0, 0), (pack_e, NXD // 128 - 1, 112)):
        for p in range(NYD // 8):
            packed = jnp.zeros((C, 128), F32)
            for j in range(8):
                cells = own[8 * p + j, :, 128 * tile : 128 * tile + 128]
                packed = jnp.where(lane // 16 == j, turn(cells, 16 * j - first), packed)
            pack[2 + p] = packed
    for pack, first in ((pack_w, 0), (pack_e, 120)):
        packed = jnp.zeros((C, 128), F32)
        for m in range(PYD):
            packed = jnp.where(lane // 8 == m, turn(pown[m], 8 * m - first), packed)
        pack[0] = packed
        pack[1] = mine
        pack[8] = packed
        pack[9] = mine

    sends = (
        (pack_e.at[pl.ds(6, 4)], corner.at[0], (1, 1)),
        (pack_w.at[pl.ds(6, 4)], corner.at[1], (-1, 1)),
        (pack_e.at[pl.ds(0, 4)], corner.at[2], (1, -1)),
        (pack_w.at[pl.ds(0, 4)], corner.at[3], (-1, -1)),
        (pack_e.at[pl.ds(0, 8)], west, (1, 0)),
        (pack_w.at[pl.ds(0, 8)], east, (-1, 0)),
        (own.at[pl.ds(NYD - H, H)], south, (0, 1)),
        (own.at[pl.ds(0, H)], north, (0, -1)),
        (pown.at[pl.ds(PYD - PH, PH)], psouth, (0, 1)),
        (pown.at[pl.ds(0, PH)], pnorth, (0, -1)),
        (info.at[0], info.at[1], (0, 1)),
        (info.at[0], info.at[2], (0, -1)),
    )
    pl.semaphore_wait(barrier, len(AROUND) - 1)
    copies = []
    for i, (source, target, (dx, dy)) in enumerate(sends):
        copy = pltpu.make_async_remote_copy(
            src_ref=source, dst_ref=target, send_sem=send_sem.at[i], recv_sem=recv_sem.at[i],
            device_id=device(dx, dy), device_id_type=MESH,
        )
        copy.start()
        copies.append(copy)
    for copy in copies:
        copy.wait()


def advance_all(tiles_x, tiles_y, diffusion, drift, own, south, north, pown, psouth, pnorth, west, east, corner, info,
                nest_out, parent_out,
                one, two, old, new, cols_old, cols_new, lines, row_g, col_g, places, out_v, sum_v, place_sem, out_sem):
    gx, gy = lax.axis_index("gx"), lax.axis_index("gy")
    lane = lanes_of((C, 128))
    notes = (info.at[0], info.at[1], info.at[2], west.at[1], east.at[1],
             corner.at[0, 3], corner.at[1, 3], corner.at[2, 1], corner.at[3, 1])
    moves = [pltpu.make_async_copy(note.at[pl.ds(0, 8)], places.at[j], place_sem.at[j]) for j, note in enumerate(notes)]
    for move in moves:
        move.start()

    has_w, has_e = (gx > 0).astype(F32), (gx < tiles_x - 1).astype(F32)
    has_s, has_n = (gy > 0).astype(F32), (gy < tiles_y - 1).astype(F32)
    of_x = {-1: has_w, 0: None, 1: has_e}
    of_y = {-1: has_s, 0: None, 1: has_n}

    push = jnp.zeros((C, 128), F32)
    scale = jnp.zeros((C, 128), F32)
    disk_rows = jnp.full((C, 128), 1.0e6, F32)
    disk_cols = jnp.full((C, 128), 1.0e6, F32)
    for j, (dx, dy) in enumerate(AROUND):
        note = notes[j][...]
        here = lane // MAXD == j
        first, force = turn(note, MAXD * j), turn(note, MAXD * j - 3 * MAXD)
        for there in (of_x[dx], of_y[dy]):
            if there is not None:
                first, force = first * there, force * there
        push = jnp.where(here, first, push)
        scale = jnp.where(here, force, scale)
        disk_rows = jnp.where(here, turn(note, MAXD * j - MAXD) + float(H + NYD * dy), disk_rows)
        disk_cols = jnp.where(here, turn(note, MAXD * j - 2 * MAXD) + float(NXD * dx), disk_cols)

    def thrice(value):
        shape = value.shape
        at = lanes_of(shape)
        later = turn(value, SLOT)
        return (jnp.where(at < SLOT, value, later),
                jnp.where(at < 2 * SLOT - 128, later, turn(value, 2 * SLOT - 128)))

    def profile(distance):
        return jnp.where(jnp.abs(distance) <= float(FOOT), jnp.exp(distance * distance * (-1.0 / 8.0)), 0.0)

    rows_2 = thrice(disk_rows[0:8])
    height = lax.broadcasted_iota(jnp.int32, (8, 128), 0).astype(F32)
    for block in range(ROWS // 8):
        for half in range(2):
            value = profile(height + float(8 * block) - rows_2[half])
            for j in range(8):
                row_g[8 * block + j, :, 128 * half : 128 * half + 128] = value[j : j + 1]
    cols_2 = thrice(disk_cols[0:8])
    depth_at = lax.broadcasted_iota(jnp.int32, (128, 128), 0)
    for half in range(2):
        across = jnp.transpose(jnp.broadcast_to(cols_2[half][0:1], (128, 128)))
        third = depth_at + 128 * half >= 2 * SLOT
        for tile in range(WIDE // 128):
            at = lanes_of((128, 128)) + 128 * tile
            at = jnp.where(at < 448, at, at - WIDE).astype(F32)
            value = profile(at - across)
            rest = value - value.astype(BF16).astype(F32)
            col_g[128 * half : 128 * half + 128, 128 * tile : 128 * tile + 128] = jnp.where(third, rest, value).astype(BF16)

    def copy_rows(source, base, count):
        def body(i, carry):
            one[base + i, :, 0:NXD] = source[i]
            return carry
        lax.fori_loop(0, count, body, 0)

    copy_rows(south, 0, H)
    copy_rows(own, H, NYD)
    copy_rows(north, H + NYD, H)
    for p in range(ROWS // 8):
        if p < 2:
            from_w, from_e = corner[0, p], corner[1, p]
        elif p < 8:
            from_w, from_e = west[p], east[p]
        else:
            from_w, from_e = corner[2, p - 6], corner[3, p - 6]
        for j in range(8):
            one[8 * p + j, :, NXD:WIDE] = jnp.where(
                lane < 16, turn(from_e, -16 * j), jnp.where(lane >= 112, turn(from_w, 112 - 16 * j), 0.0))

    plane = lax.broadcasted_iota(jnp.int32, (C, 128), 0)

    def per_plane(read):
        value = jnp.zeros((C, 128), F32)
        for c in range(C):
            value = jnp.where(plane == c, read(c), value)
        return value

    spread = per_plane(lambda c: diffusion[c])
    east_by = per_plane(lambda c: drift[0, c])
    north_by = per_plane(lambda c: drift[1, c])

    def stencil(a):
        return (1.0 - 4.0 * a - east_by - north_by, a + east_by, a, a + north_by, a)

    def shifted(tiles):
        count = len(tiles)
        up = [turn(v, 1) for v in tiles]
        down = [turn(v, -1) for v in tiles]
        from_w = [jnp.where(lane == 0, up[(t - 1) % count], up[t]) for t in range(count)]
        from_e = [jnp.where(lane == 127, down[(t + 1) % count], down[t]) for t in range(count)]
        return from_w, from_e

    for block, (source, there, strips) in enumerate((
        (psouth, has_s, (corner[0, 2], corner[1, 2], 8)),
        (pown, None, (west[0], east[0], 0)),
        (pnorth, has_n, (corner[2, 0], corner[3, 0], 0)),
    )):
        base = (0, PH, PH + PYD)[block]
        count = (PH, PYD, PH)[block]
        for i in range(count):
            middle = source[i]
            m = i + strips[2]
            side = jnp.where(lane < 8, turn(strips[1], -8 * m) * has_e,
                             jnp.where(lane >= 120, turn(strips[0], 120 - 8 * m) * has_w, 0.0))
            if there is not None:
                middle, side = middle * there, side * there
            old[base + i, :, 0:128] = middle
            old[base + i, :, 128:256] = side
    kept = jnp.where(lane < 64, has_e, has_w)
    stay, cw, ce, cs, cn = stencil(spread * (1.0 / 3.0))
    new[0] = jnp.zeros((C, PWIDE), F32)
    new[PROWS - 1] = jnp.zeros((C, PWIDE), F32)

    def parent_row(i, carry):
        inside = jnp.where(i < PH, has_s, jnp.where(i >= PH + PYD, has_n, 1.0))
        tiles = [old[i, :, 128 * t : 128 * t + 128] for t in range(2)]
        from_w, from_e = shifted(tiles)
        for t in range(2):
            value = (stay * tiles[t] + cw * from_w[t] + ce * from_e[t]
                     + cs * old[i - 1, :, 128 * t : 128 * t + 128] + cn * old[i + 1, :, 128 * t : 128 * t + 128])
            value = value * inside
            new[i, :, 128 * t : 128 * t + 128] = value * kept if t == 1 else value
        return carry

    lax.fori_loop(1, PROWS - 1, parent_row, 0)

    @pl.when((gx == 0) | (gx == tiles_x - 1))
    def _():
        for source, target in ((old, cols_old), (new, cols_new)):
            for y in range(ROWS):
                q, rest = (y - H) // 3 + PH, (y - H) % 3
                centre = source[q, :, 0:128]
                if rest == 1:
                    value = centre * (2.0 / 3.0)
                else:
                    value = centre * (4.0 / 9.0) + source[q - 1 if rest == 0 else q + 1, :, 0:128] * (2.0 / 9.0)
                target[y] = value

    def pieces(value, count):
        out = []
        for _ in range(count):
            part = value.astype(BF16)
            out.append(part)
            value = value - part.astype(F32)
        return out

    @pl.when((gy == 0) | (gy == tiles_y - 1))
    def _():
        fine = lanes_of((PWIDE, WIDE))
        fine = jnp.where(fine < 448, fine, fine - WIDE)
        coarse = lax.broadcasted_iota(jnp.int32, (PWIDE, WIDE), 0)
        coarse = jnp.where(coarse < 192, coarse, coarse - PWIDE)
        hat = jnp.maximum(3 - jnp.abs(fine - (3 * coarse + 1)), 0).astype(F32).astype(BF16)
        at = jnp.where(gy == 0, PH, PH + PYD - 1)
        parts = pieces(old[at], 3) + pieces(new[at], 3)
        for i in range(2):
            total = jnp.zeros((C, WIDE), F32)
            for part in parts[3 * i : 3 * i + 3]:
                total = total + jnp.dot(part, hat, preferred_element_type=F32)
            lines[i] = total * (2.0 / 9.0)

    stay, cw, ce, cs, cn = stencil(spread)
    second = [lane + 128 * half for half in range(2)]
    second = [(at >= SLOT) & (at < 2 * SLOT) for at in second]

    def step(source, target, amounts, low, high, k):
        amounts_2 = thrice(amounts)

        def body(i, carry):
            base = low + CHUNK * i
            left = []
            for r in range(CHUNK):
                halves = []
                for half in range(2):
                    value = amounts_2[half] * row_g[base + r, :, 128 * half : 128 * half + 128]
                    rest = value - value.astype(BF16).astype(F32)
                    halves.append(jnp.where(second[half], rest, value).astype(BF16))
                left.append(jnp.concatenate(halves, axis=1))
            force = jnp.dot(jnp.concatenate(left, axis=0), col_g[...], preferred_element_type=F32)
            for r in range(CHUNK):
                y = base + r
                tiles = [source[y, :, 128 * t : 128 * t + 128] for t in range(4)]
                from_w, from_e = shifted(tiles)
                for t in range(4):
                    at = slice(128 * t, 128 * t + 128)
                    target[y, :, at] = (
                        stay * tiles[t] + cw * from_w[t] + ce * from_e[t] + cs * source[y - 1, :, at]
                        + cn * source[y + 1, :, at] + force[C * r : C * r + C, at])
            return carry

        lax.fori_loop(0, (high - low) // CHUNK, body, 0)

        for edge, tile, spot in ((0, 0, 0), (tiles_x - 1, NXD // 128 - 1, 127)):
            @pl.when(gx == edge)
            def _():
                def patch(i, carry):
                    at = slice(128 * tile, 128 * tile + 128)
                    bound = cols_old[i] + (k / 3.0) * (cols_new[i] - cols_old[i])
                    target[i, :, at] = jnp.where(lane == spot, bound, target[i, :, at])
                    return carry
                lax.fori_loop(low, high, patch, 0)
        for edge, row in ((0, H), (tiles_y - 1, H + NYD - 1)):
            @pl.when(gy == edge)
            def _():
                target[row] = lines[0] + (k / 3.0) * (lines[1] - lines[0])

    def gathered(source):
        wind = jnp.zeros((C, 128), F32)
        for j, (dx, dy) in enumerate(AROUND):
            for s in range(MAXD):
                d = MAXD * j + s
                row = places[j, 0, MAXD + s].astype(jnp.int32) + (H + NYD * dy)
                col = places[j, 0, 2 * MAXD + s].astype(jnp.int32) + NXD * dx
                row = jnp.clip(row, 0, ROWS - 1)
                col = jnp.bitwise_and(col, WIDE - 1)
                tile = pl.multiple_of(jnp.bitwise_and(col, WIDE - 128), 128)
                cells = source[row, :, pl.ds(tile, 128)]
                wind = jnp.where(lane == d, turn(cells, jnp.bitwise_and(d - col, 127)), wind)
        return wind

    for buffer, rows in ((two, (0, ROWS - 1)),):
        for row in rows:
            buffer[row] = jnp.zeros((C, WIDE), F32)

    step(one, two, push, 1, ROWS - 1, 1)
    for move in moves:
        move.wait()
    push = thrusts(gathered(two), scale)
    step(two, one, push, 7, ROWS - 7, 2)
    push = thrusts(gathered(one), scale)
    step(one, two, push, 13, ROWS - 13, 3)

    stores = [pltpu.make_async_copy(two.at[pl.ds(H, NYD), c, pl.ds(0, NXD)], nest_out.at[c], out_sem.at[c]) for c in range(C)]
    for store in stores:
        store.start()

    low_side = jnp.where(gx == 0, 0, -64)
    high_side = jnp.where(gx == tiles_x - 1, NXD, NXD + 64)
    fine = lax.broadcasted_iota(jnp.int32, (WIDE, 128), 0)
    fine = jnp.where(fine < 448, fine, fine - WIDE)
    gap = jnp.abs(fine - (3 * lanes_of((WIDE, 128)) + 1))
    weight = jnp.where(gap <= 1, 2.0, jnp.where(gap <= 4, 1.0, 0.0))
    weight = jnp.where((fine >= low_side) & (fine < high_side), weight, 0.0).astype(BF16)

    def three(m):
        y = H + 3 * m
        return two[y] + two[y + 1] + two[y + 2]

    before, here = three(-1) * has_s, three(0)
    high_part, low_part = [], []
    for m in range(PYD):
        after = three(m + 1)
        if m == PYD - 1:
            after = after * has_n
        total = before + 2.0 * here + after
        part = pieces(total, 2)
        sum_v[C * m : C * m + C] = part[0]
        sum_v[C * (PYD + m) : C * (PYD + m) + C] = part[1]
        before, here = here, after
    mean = jnp.dot(sum_v[...], weight, preferred_element_type=F32)
    half = C * PYD
    for m in range(PYD):
        i = m + PH
        tiles = [new[i - 1, :, 128 * t : 128 * t + 128] + 2.0 * new[i, :, 128 * t : 128 * t + 128]
                 + new[i + 1, :, 128 * t : 128 * t + 128] for t in range(2)]
        from_w, from_e = shifted(tiles)
        direct = from_w[0] + 2.0 * tiles[0] + from_e[0]
        out_v[m] = direct * (1.0 / 32.0) + (mean[C * m : C * m + C] + mean[half + C * m : half + C * m + C]) * (1.0 / 288.0)
    last = [pltpu.make_async_copy(out_v.at[:, c, :], parent_out.at[c], out_sem.at[C + c]) for c in range(C)]
    for store in last:
        store.start()
    for store in stores + last:
        store.wait()


def solution(mesh):
    tiles_x, tiles_y = mesh.shape["gx"], mesh.shape["gy"]
    smem = pl.BlockSpec(memory_space=pltpu.SMEM)
    vmem = pl.BlockSpec(memory_space=pltpu.VMEM)
    anywhere = pl.BlockSpec(memory_space=pl.ANY)
    passed = ((NYD, C, NXD), (H, C, NXD), (H, C, NXD), (PYD, C, PXD), (PH, C, PXD), (PH, C, PXD),
              (8, C, 128), (8, C, 128), (4, 4, C, 128), (3, C, 128))

    def on_device(nest_wind, parent_wind, diffusion, drift, disk_sites, disk_live, disk_coef):
        rims = pl.pallas_call(
            functools.partial(exchange, tiles_x, tiles_y),
            out_shape=[pltpu.VMEM(shape, F32) for shape in passed],
            in_specs=[anywhere, anywhere, smem, smem, smem],
            out_specs=[vmem] * len(passed),
            scratch_shapes=[
                pltpu.VMEM((10, C, 128), F32),
                pltpu.VMEM((10, C, 128), F32),
                pltpu.SemaphoreType.DMA((2 * C,)),
                pltpu.SemaphoreType.DMA((12,)),
                pltpu.SemaphoreType.DMA((12,)),
            ],
            compiler_params=pltpu.CompilerParams(
                collective_id=0, has_side_effects=True, vmem_limit_bytes=16 * 2**20),
            name="exchange",
        )(nest_wind, parent_wind, disk_sites, disk_live, disk_coef)
        return tuple(pl.pallas_call(
            functools.partial(advance_all, tiles_x, tiles_y),
            out_shape=[jax.ShapeDtypeStruct(nest_wind.shape, F32), jax.ShapeDtypeStruct(parent_wind.shape, F32)],
            in_specs=[smem, smem] + [vmem] * len(passed),
            out_specs=[anywhere, anywhere],
            scratch_shapes=[
                pltpu.VMEM((ROWS, C, WIDE), F32),
                pltpu.VMEM((ROWS, C, WIDE), F32),
                pltpu.VMEM((PROWS, C, PWIDE), F32),
                pltpu.VMEM((PROWS, C, PWIDE), F32),
                pltpu.VMEM((ROWS, C, 128), F32),
                pltpu.VMEM((ROWS, C, 128), F32),
                pltpu.VMEM((2, C, WIDE), F32),
                pltpu.VMEM((ROWS, 1, 256), F32),
                pltpu.VMEM((256, WIDE), BF16),
                pltpu.SMEM((9, 8, 128), F32),
                pltpu.VMEM((PYD, C, PXD), F32),
                pltpu.VMEM((2 * C * PYD, WIDE), BF16),
                pltpu.SemaphoreType.DMA((9,)),
                pltpu.SemaphoreType.DMA((2 * C,)),
            ],
            compiler_params=pltpu.CompilerParams(vmem_limit_bytes=40 * 2**20),
            name="advance",
        )(diffusion, drift, *rims))

    placed = (
        P(None, "gy", "gx"),
        P(None, "gy", "gx"),
        P(),
        P(),
        P(None, "gy", "gx", None),
        P("gy", "gx", None),
        P("gy", "gx", None),
    )
    return jax.shard_map(
        on_device,
        mesh=mesh,
        in_specs=placed,
        out_specs=(P(None, "gy", "gx"), P(None, "gy", "gx")),
        check_vma=False,
    )
```

```python
import functools

import jax
import jax.numpy as jnp
from jax import lax
from jax.experimental import pallas as pl
from jax.experimental.pallas import tpu as pltpu
from jax.sharding import PartitionSpec as P

C = 16
NYD = 48
NXD = 384
PYD = 16
PXD = 128
MAXD = 8
FOOT = 6
H = 16
PH = 8
NEAR = 6
PNEAR = 2
ROWS = NYD + 2 * H
PROWS = PYD + 2 * PH
WIDE = 512
PWIDE = 256
SLOT = 80
CHUNK = 6
F32 = jnp.float32
BF16 = jnp.bfloat16
MESH = pl.DeviceIdType.MESH
AROUND = ((0, 0), (0, -1), (0, 1), (-1, 0), (1, 0), (-1, -1), (1, -1), (-1, 1), (1, 1))


def lanes_of(shape):
    return lax.broadcasted_iota(jnp.int32, shape, len(shape) - 1)


def turn(value, shift):
    shift = shift % value.shape[-1] if isinstance(shift, int) else shift
    if isinstance(shift, int) and shift == 0:
        return value
    return pltpu.roll(value, shift, value.ndim - 1)


def thrusts(wind, scale):
    half = C // 2
    east, north = wind[:half], wind[half:]
    speed = jnp.sqrt(east * east + north * north + 1.0)
    return scale * wind * jnp.concatenate([speed, speed], axis=0)


def plane_tile(read):
    at = lax.broadcasted_iota(jnp.int32, (C, 128), 0)
    value = jnp.zeros((C, 128), F32)
    for c in range(C):
        value = jnp.where(at == c, read(c), value)
    return value


def factors(spread, east_by, north_by):
    return (1.0 - 4.0 * spread - east_by - north_by, spread + east_by, spread, spread + north_by, spread)


def exchange(tiles_x, tiles_y, nest, parent, diffusion_h, drift_h, sites_h, live_h, coef_h,
             own, south, north, pown, psouth, pnorth, west, east, corner, info, sides,
             pack_w, pack_e, diffusion, drift, sites, live, coef, in_sem, send_sem, recv_sem):
    gx, gy = lax.axis_index("gx"), lax.axis_index("gy")

    def device(dx, dy):
        return (lax.rem(gx + dx + tiles_x, tiles_x), lax.rem(gy + dy + tiles_y, tiles_y))

    barrier = pltpu.get_barrier_semaphore()
    for dx, dy in AROUND[1:]:
        pl.semaphore_signal(barrier, inc=1, device_id=device(dx, dy), device_id_type=MESH)

    small = ((diffusion_h, diffusion), (drift_h, drift), (sites_h, sites), (live_h, live), (coef_h, coef))
    loads = [pltpu.make_async_copy(nest.at[c], own.at[:, c, :], in_sem.at[c]) for c in range(C)]
    loads += [pltpu.make_async_copy(parent.at[c], pown.at[:, c, :], in_sem.at[C + c]) for c in range(C)]
    loads += [pltpu.make_async_copy(a, b, in_sem.at[2 * C + i]) for i, (a, b) in enumerate(small)]
    for load in loads:
        load.start()
    for load in loads:
        load.wait()

    lane = lanes_of((C, PXD))
    for pack, tile, first in ((pack_w, 0, 0), (pack_e, NXD // 128 - 1, 112)):
        for p in range(NYD // 8):
            packed = jnp.zeros((C, 128), F32)
            for j in range(8):
                cells = own[8 * p + j, :, 128 * tile : 128 * tile + 128]
                packed = jnp.where(lane // 16 == j, turn(cells, 16 * j - first), packed)
            pack[2 + p] = packed
    for pack, first in ((pack_w, 0), (pack_e, 120)):
        packed = jnp.zeros((C, 128), F32)
        for m in range(PYD):
            packed = jnp.where(lane // 8 == m, turn(pown[m], 8 * m - first), packed)
        pack[0] = packed
        pack[8] = packed

    wide_lane = lanes_of((C, NXD))
    inner = (wide_lane >= H) & (wide_lane < NXD - H)
    stay, cw, ce, cs, cn = factors(
        plane_tile(lambda c: diffusion[c]), plane_tile(lambda c: drift[0, c]), plane_tile(lambda c: drift[1, c]))
    middle = stay * stay + 2.0 * (cw * ce + cs * cn)

    def three(value):
        return jnp.concatenate([value] * (NXD // 128), axis=1)

    row_weights = [three(v) for v in (cw, stay, ce)]
    square_weights = [three(v) for v in (cw * cw, 2.0 * cw * stay, middle, 2.0 * stay * ce, ce * ce)]
    wind = jnp.zeros((C, PXD), F32)
    scale = jnp.zeros((C, PXD), F32)
    spot = jnp.zeros((C, PXD), F32)
    rests = [jnp.zeros((C, PXD), F32)] * 2

    def total(value):
        return jnp.sum(value, axis=1, keepdims=True)

    for s in range(MAXD):
        row, col = sites[0, 0, 0, s], sites[1, 0, 0, s]
        gap = wide_lane - col
        at_0 = gap == 0
        value = total(jnp.where(at_0, own[row], 0.0))
        wind = jnp.where(lane == s, value, wind)
        push = -(coef[0, 0, s] * live[0, 0, s].astype(F32))
        scale = jnp.where(lane == s, push, scale)
        spot = jnp.where(lane == MAXD + s, row.astype(F32), spot)
        spot = jnp.where(lane == 2 * MAXD + s, col.astype(F32), spot)
        spot = jnp.where(lane == 3 * MAXD + s, push, spot)
        line = jnp.where(gap == -1, row_weights[0], jnp.where(at_0, row_weights[1], jnp.where(gap == 1, row_weights[2], 0.0)))
        square = jnp.zeros((C, NXD), F32)
        for j in range(5):
            square = jnp.where(gap == j - 2, square_weights[j], square)
        near = {r: jnp.where(inner, own[jnp.clip(row + r, 0, NYD - 1)], 0.0) for r in range(-2, 3)}
        along = {r: total(line * near[r]) for r in range(-1, 2)}
        point = {r: total(jnp.where(at_0, near[r], 0.0)) for r in (-2, -1, 1, 2)}
        ones = {0: along[0], -1: cs * point[-1], 1: cn * point[1]}
        twos = {0: total(square * near[0]), -1: 2.0 * cs * along[-1], 1: 2.0 * cn * along[1],
                -2: cs * cs * point[-2], 2: cn * cn * point[2]}
        for way, (low, high) in enumerate(((NEAR, NYD - 1), (0, NYD - 1 - NEAR))):
            for terms, at in ((ones, 4 * MAXD + s), (twos, 5 * MAXD + s)):
                value = jnp.zeros((C, 128), F32)
                for r, term in terms.items():
                    value = value + term * ((row + r >= low) & (row + r <= high)).astype(F32)
                rests[way] = jnp.where(lane == at, value, rests[way])
    mine = thrusts(wind, scale) + spot
    info[0] = mine
    for pack in (pack_w, pack_e):
        pack[1] = mine
        pack[9] = mine
    for way in range(2):
        base = 10 + 7 * way
        for i in range(2):
            first = 2 + i if way == 0 else 6 + i
            pack_w[base + i] = pack_w[first]
            pack_w[base + 2 + i] = pack_e[first]
        pack_w[base + 4] = pack_w[0]
        pack_w[base + 5] = pack_e[0]
        pack_w[base + 6] = mine + rests[way]

    sends = (
        (pack_e.at[pl.ds(6, 4)], corner.at[0], (1, 1)),
        (pack_w.at[pl.ds(6, 4)], corner.at[1], (-1, 1)),
        (pack_e.at[pl.ds(0, 4)], corner.at[2], (1, -1)),
        (pack_w.at[pl.ds(0, 4)], corner.at[3], (-1, -1)),
        (pack_e.at[pl.ds(0, 8)], west, (1, 0)),
        (pack_w.at[pl.ds(0, 8)], east, (-1, 0)),
        (own.at[pl.ds(NYD - NEAR, NEAR)], south, (0, 1)),
        (own.at[pl.ds(0, NEAR)], north, (0, -1)),
        (pown.at[pl.ds(PYD - PNEAR, PNEAR)], psouth, (0, 1)),
        (pown.at[pl.ds(0, PNEAR)], pnorth, (0, -1)),
        (pack_w.at[pl.ds(17, 7)], sides.at[0], (0, 1)),
        (pack_w.at[pl.ds(10, 7)], sides.at[1], (0, -1)),
    )
    pl.semaphore_wait(barrier, len(AROUND) - 1)
    copies = []
    for i, (source, target, (dx, dy)) in enumerate(sends):
        copy = pltpu.make_async_remote_copy(
            src_ref=source, dst_ref=target, send_sem=send_sem.at[i], recv_sem=recv_sem.at[i],
            device_id=device(dx, dy), device_id_type=MESH,
        )
        copy.start()
        copies.append(copy)
    for copy in copies:
        copy.wait()


def advance_all(tiles_x, tiles_y, diffusion, drift, own, south, north, pown, psouth, pnorth, west, east, corner, info, sides,
                nest_out, parent_out,
                one, two, old, new, cols_old, cols_new, lines, row_g, col_g, places, out_v, sum_v, place_sem, out_sem):
    gx, gy = lax.axis_index("gx"), lax.axis_index("gy")
    lane = lanes_of((C, 128))
    notes = (info.at[0], sides.at[0, 6], sides.at[1, 6], west.at[1], east.at[1],
             corner.at[0, 3], corner.at[1, 3], corner.at[2, 1], corner.at[3, 1])
    moves = [pltpu.make_async_copy(note.at[pl.ds(0, 8)], places.at[j], place_sem.at[j]) for j, note in enumerate(notes)]
    for move in moves:
        move.start()

    has_w, has_e = (gx > 0).astype(F32), (gx < tiles_x - 1).astype(F32)
    has_s, has_n = (gy > 0).astype(F32), (gy < tiles_y - 1).astype(F32)
    of_x = {-1: has_w, 0: None, 1: has_e}
    of_y = {-1: has_s, 0: None, 1: has_n}

    push = jnp.zeros((C, 128), F32)
    scale = jnp.zeros((C, 128), F32)
    disk_rows = jnp.full((C, 128), 1.0e6, F32)
    disk_cols = jnp.full((C, 128), 1.0e6, F32)
    missing = [jnp.zeros((C, 128), F32)] * 2
    for j, (dx, dy) in enumerate(AROUND):
        note = notes[j][...]
        here = lane // MAXD == j
        first, force = turn(note, MAXD * j), turn(note, MAXD * j - 3 * MAXD)
        for there in (of_x[dx], of_y[dy]):
            if there is not None:
                first, force = first * there, force * there
        if dx == 0 and dy != 0:
            missing = [jnp.where(here, turn(note, MAXD * j - (4 + i) * MAXD), missing[i]) for i in range(2)]
        push = jnp.where(here, first, push)
        scale = jnp.where(here, force, scale)
        disk_rows = jnp.where(here, turn(note, MAXD * j - MAXD) + float(H + NYD * dy), disk_rows)
        disk_cols = jnp.where(here, turn(note, MAXD * j - 2 * MAXD) + float(NXD * dx), disk_cols)

    def thrice(value):
        shape = value.shape
        at = lanes_of(shape)
        later = turn(value, SLOT)
        return (jnp.where(at < SLOT, value, later),
                jnp.where(at < 2 * SLOT - 128, later, turn(value, 2 * SLOT - 128)))

    def profile(distance):
        return jnp.where(jnp.abs(distance) <= float(FOOT), jnp.exp(distance * distance * (-1.0 / 8.0)), 0.0)

    rows_2 = thrice(disk_rows[0:8])
    height = lax.broadcasted_iota(jnp.int32, (8, 128), 0).astype(F32)
    for block in range(ROWS // 8):
        for half in range(2):
            value = profile(height + float(8 * block) - rows_2[half])
            for j in range(8):
                row_g[8 * block + j, :, 128 * half : 128 * half + 128] = value[j : j + 1]
    cols_2 = thrice(disk_cols[0:8])
    depth_at = lax.broadcasted_iota(jnp.int32, (128, 128), 0)
    for half in range(2):
        across = jnp.transpose(jnp.broadcast_to(cols_2[half][0:1], (128, 128)))
        third = depth_at + 128 * half >= 2 * SLOT
        for tile in range(WIDE // 128):
            at = lanes_of((128, 128)) + 128 * tile
            at = jnp.where(at < 448, at, at - WIDE).astype(F32)
            value = profile(at - across)
            rest = value - value.astype(BF16).astype(F32)
            col_g[128 * half : 128 * half + 128, 128 * tile : 128 * tile + 128] = jnp.where(third, rest, value).astype(BF16)

    def copy_rows(source, base, count):
        def body(i, carry):
            one[base + i, :, 0:NXD] = source[i]
            return carry
        lax.fori_loop(0, count, body, 0)

    copy_rows(south, H - NEAR, NEAR)
    copy_rows(own, H, NYD)
    copy_rows(north, H + NYD, NEAR)
    for p in range(ROWS // 8):
        if p < 2:
            from_w, from_e = corner[0, p], corner[1, p]
        elif p < 8:
            from_w, from_e = west[p], east[p]
        else:
            from_w, from_e = corner[2, p - 6], corner[3, p - 6]
        for j in range(8):
            y = 8 * p + j
            one[y, :, NXD:WIDE] = jnp.where(
                lane < 16, turn(from_e, -16 * j), jnp.where(lane >= 112, turn(from_w, 112 - 16 * j), 0.0))
            if y < H - NEAR or y >= H + NYD + NEAR:
                way, i = (0, p) if y < H else (1, p - 8)
                one[y, :, 0:128] = jnp.where(lane < 16, turn(sides[way, i], -16 * j), 0.0)
                one[y, :, 128 : NXD - 128] = jnp.zeros((C, NXD - 256), F32)
                one[y, :, NXD - 128 : NXD] = jnp.where(lane >= 112, turn(sides[way, 2 + i], 112 - 16 * j), 0.0)

    spread = plane_tile(lambda c: diffusion[c])
    east_by = plane_tile(lambda c: drift[0, c])
    north_by = plane_tile(lambda c: drift[1, c])

    def shifted(tiles):
        count = len(tiles)
        up = [turn(v, 1) for v in tiles]
        down = [turn(v, -1) for v in tiles]
        from_w = [jnp.where(lane == 0, up[(t - 1) % count], up[t]) for t in range(count)]
        from_e = [jnp.where(lane == 127, down[(t + 1) % count], down[t]) for t in range(count)]
        return from_w, from_e

    for block, (source, there, strips) in enumerate((
        (psouth, has_s, (corner[0, 2], corner[1, 2], 8)),
        (pown, None, (west[0], east[0], 0)),
        (pnorth, has_n, (corner[2, 0], corner[3, 0], 0)),
    )):
        base = (0, PH, PH + PYD)[block]
        count = (PH, PYD, PH)[block]
        for i in range(count):
            m = i + strips[2]
            if block == 0 and i < PH - PNEAR or block == 2 and i >= PNEAR:
                way = block // 2
                middle = jnp.where(lane < 8, turn(sides[way, 4], -8 * m),
                                   jnp.where(lane >= 120, turn(sides[way, 5], 120 - 8 * m), 0.0))
            else:
                middle = source[i - (PH - PNEAR) if block == 0 else i]
            side = jnp.where(lane < 8, turn(strips[1], -8 * m) * has_e,
                             jnp.where(lane >= 120, turn(strips[0], 120 - 8 * m) * has_w, 0.0))
            if there is not None:
                middle, side = middle * there, side * there
            old[base + i, :, 0:128] = middle
            old[base + i, :, 128:256] = side
    kept = jnp.where(lane < 64, has_e, has_w)
    stay, cw, ce, cs, cn = factors(spread * (1.0 / 3.0), east_by, north_by)
    new[0] = jnp.zeros((C, PWIDE), F32)
    new[PROWS - 1] = jnp.zeros((C, PWIDE), F32)

    def parent_row(i, carry):
        inside = jnp.where(i < PH, has_s, jnp.where(i >= PH + PYD, has_n, 1.0))
        tiles = [old[i, :, 128 * t : 128 * t + 128] for t in range(2)]
        from_w, from_e = shifted(tiles)
        for t in range(2):
            value = (stay * tiles[t] + cw * from_w[t] + ce * from_e[t]
                     + cs * old[i - 1, :, 128 * t : 128 * t + 128] + cn * old[i + 1, :, 128 * t : 128 * t + 128])
            value = value * inside
            new[i, :, 128 * t : 128 * t + 128] = value * kept if t == 1 else value
        return carry

    lax.fori_loop(1, PROWS - 1, parent_row, 0)

    @pl.when((gx == 0) | (gx == tiles_x - 1))
    def _():
        for source, target in ((old, cols_old), (new, cols_new)):
            for y in range(ROWS):
                q, rest = (y - H) // 3 + PH, (y - H) % 3
                centre = source[q, :, 0:128]
                if rest == 1:
                    value = centre * (2.0 / 3.0)
                else:
                    value = centre * (4.0 / 9.0) + source[q - 1 if rest == 0 else q + 1, :, 0:128] * (2.0 / 9.0)
                target[y] = value

    def pieces(value, count):
        out = []
        for _ in range(count):
            part = value.astype(BF16)
            out.append(part)
            value = value - part.astype(F32)
        return out

    @pl.when((gy == 0) | (gy == tiles_y - 1))
    def _():
        fine = lanes_of((PWIDE, WIDE))
        fine = jnp.where(fine < 448, fine, fine - WIDE)
        coarse = lax.broadcasted_iota(jnp.int32, (PWIDE, WIDE), 0)
        coarse = jnp.where(coarse < 192, coarse, coarse - PWIDE)
        hat = jnp.maximum(3 - jnp.abs(fine - (3 * coarse + 1)), 0).astype(F32).astype(BF16)
        at = jnp.where(gy == 0, PH, PH + PYD - 1)
        parts = pieces(old[at], 3) + pieces(new[at], 3)
        for i in range(2):
            total = jnp.zeros((C, WIDE), F32)
            for part in parts[3 * i : 3 * i + 3]:
                total = total + jnp.dot(part, hat, preferred_element_type=F32)
            lines[i] = total * (2.0 / 9.0)

    stay, cw, ce, cs, cn = factors(spread, east_by, north_by)
    second = [lane + 128 * half for half in range(2)]
    second = [(at >= SLOT) & (at < 2 * SLOT) for at in second]

    def step(source, target, amounts, low, high, k):
        amounts_2 = thrice(amounts)

        def body(i, carry):
            base = low + CHUNK * i
            left = []
            for r in range(CHUNK):
                halves = []
                for half in range(2):
                    value = amounts_2[half] * row_g[base + r, :, 128 * half : 128 * half + 128]
                    rest = value - value.astype(BF16).astype(F32)
                    halves.append(jnp.where(second[half], rest, value).astype(BF16))
                left.append(jnp.concatenate(halves, axis=1))
            force = jnp.dot(jnp.concatenate(left, axis=0), col_g[...], preferred_element_type=F32)
            for r in range(CHUNK):
                y = base + r
                tiles = [source[y, :, 128 * t : 128 * t + 128] for t in range(4)]
                from_w, from_e = shifted(tiles)
                for t in range(4):
                    at = slice(128 * t, 128 * t + 128)
                    target[y, :, at] = (
                        stay * tiles[t] + cw * from_w[t] + ce * from_e[t] + cs * source[y - 1, :, at]
                        + cn * source[y + 1, :, at] + force[C * r : C * r + C, at])
            return carry

        lax.fori_loop(0, (high - low) // CHUNK, body, 0, unroll=True)

        for edge, tile, spot in ((0, 0, 0), (tiles_x - 1, NXD // 128 - 1, 127)):
            @pl.when(gx == edge)
            def _():
                def patch(i, carry):
                    at = slice(128 * tile, 128 * tile + 128)
                    bound = cols_old[i] + (k / 3.0) * (cols_new[i] - cols_old[i])
                    target[i, :, at] = jnp.where(lane == spot, bound, target[i, :, at])
                    return carry
                lax.fori_loop(low, high, patch, 0)
        for edge, row in ((0, H), (tiles_y - 1, H + NYD - 1)):
            @pl.when(gy == edge)
            def _():
                target[row] = lines[0] + (k / 3.0) * (lines[1] - lines[0])

    def gathered(source):
        wind = jnp.zeros((C, 128), F32)
        for j, (dx, dy) in enumerate(AROUND):
            for s in range(MAXD):
                d = MAXD * j + s
                row = places[j, 0, MAXD + s].astype(jnp.int32) + (H + NYD * dy)
                col = places[j, 0, 2 * MAXD + s].astype(jnp.int32) + NXD * dx
                row = jnp.clip(row, 0, ROWS - 1)
                col = jnp.bitwise_and(col, WIDE - 1)
                tile = pl.multiple_of(jnp.bitwise_and(col, WIDE - 128), 128)
                cells = source[row, :, pl.ds(tile, 128)]
                wind = jnp.where(lane == d, turn(cells, jnp.bitwise_and(d - col, 127)), wind)
        return wind

    for buffer, rows in ((two, (0, ROWS - 1)),):
        for row in rows:
            buffer[row] = jnp.zeros((C, WIDE), F32)

    step(one, two, push, 1, ROWS - 1, 1)
    for move in moves:
        move.wait()
    push = thrusts(gathered(two) + missing[0], scale)
    step(two, one, push, 7, ROWS - 7, 2)
    push = thrusts(gathered(one) + missing[1], scale)
    step(one, two, push, 13, ROWS - 13, 3)

    stores = [pltpu.make_async_copy(two.at[pl.ds(H, NYD), c, pl.ds(0, NXD)], nest_out.at[c], out_sem.at[c]) for c in range(C)]
    for store in stores:
        store.start()

    low_side = jnp.where(gx == 0, 0, -64)
    high_side = jnp.where(gx == tiles_x - 1, NXD, NXD + 64)
    fine = lax.broadcasted_iota(jnp.int32, (WIDE, 128), 0)
    fine = jnp.where(fine < 448, fine, fine - WIDE)
    gap = jnp.abs(fine - (3 * lanes_of((WIDE, 128)) + 1))
    weight = jnp.where(gap <= 1, 2.0, jnp.where(gap <= 4, 1.0, 0.0))
    weight = jnp.where((fine >= low_side) & (fine < high_side), weight, 0.0).astype(BF16)

    def three(m):
        y = H + 3 * m
        return two[y] + two[y + 1] + two[y + 2]

    before, here = three(-1) * has_s, three(0)
    high_part, low_part = [], []
    for m in range(PYD):
        after = three(m + 1)
        if m == PYD - 1:
            after = after * has_n
        total = before + 2.0 * here + after
        part = pieces(total, 2)
        sum_v[C * m : C * m + C] = part[0]
        sum_v[C * (PYD + m) : C * (PYD + m) + C] = part[1]
        before, here = here, after
    mean = jnp.dot(sum_v[...], weight, preferred_element_type=F32)
    half = C * PYD
    for m in range(PYD):
        i = m + PH
        tiles = [new[i - 1, :, 128 * t : 128 * t + 128] + 2.0 * new[i, :, 128 * t : 128 * t + 128]
                 + new[i + 1, :, 128 * t : 128 * t + 128] for t in range(2)]
        from_w, from_e = shifted(tiles)
        direct = from_w[0] + 2.0 * tiles[0] + from_e[0]
        out_v[m] = direct * (1.0 / 32.0) + (mean[C * m : C * m + C] + mean[half + C * m : half + C * m + C]) * (1.0 / 288.0)
    last = [pltpu.make_async_copy(out_v.at[:, c, :], parent_out.at[c], out_sem.at[C + c]) for c in range(C)]
    for store in last:
        store.start()
    for store in stores + last:
        store.wait()


def solution(mesh):
    tiles_x, tiles_y = mesh.shape["gx"], mesh.shape["gy"]
    smem = pl.BlockSpec(memory_space=pltpu.SMEM)
    vmem = pl.BlockSpec(memory_space=pltpu.VMEM)
    anywhere = pl.BlockSpec(memory_space=pl.ANY)
    passed = ((NYD, C, NXD), (NEAR, C, NXD), (NEAR, C, NXD), (PYD, C, PXD), (PNEAR, C, PXD), (PNEAR, C, PXD),
              (8, C, 128), (8, C, 128), (4, 4, C, 128), (1, C, 128), (2, 7, C, 128))

    def on_device(nest_wind, parent_wind, diffusion, drift, disk_sites, disk_live, disk_coef):
        rims = pl.pallas_call(
            functools.partial(exchange, tiles_x, tiles_y),
            out_shape=[pltpu.VMEM(shape, F32) for shape in passed],
            in_specs=[pl.BlockSpec(memory_space=pltpu.HBM)] * 7,
            out_specs=[vmem] * len(passed),
            scratch_shapes=[
                pltpu.VMEM((24, C, 128), F32),
                pltpu.VMEM((10, C, 128), F32),
                pltpu.SMEM(diffusion.shape, F32),
                pltpu.SMEM(drift.shape, F32),
                pltpu.SMEM((2, 1, 1, MAXD), jnp.int32),
                pltpu.SMEM((1, 1, MAXD), jnp.int32),
                pltpu.SMEM((1, 1, MAXD), F32),
                pltpu.SemaphoreType.DMA((2 * C + 5,)),
                pltpu.SemaphoreType.DMA((12,)),
                pltpu.SemaphoreType.DMA((12,)),
            ],
            compiler_params=pltpu.CompilerParams(
                collective_id=0, has_side_effects=True, vmem_limit_bytes=16 * 2**20),
            name="exchange",
        )(*[pltpu.with_memory_space_constraint(x, pltpu.HBM) for x in
            (nest_wind, parent_wind, diffusion, drift, disk_sites, disk_live, disk_coef)])
        return tuple(pl.pallas_call(
            functools.partial(advance_all, tiles_x, tiles_y),
            out_shape=[jax.ShapeDtypeStruct(nest_wind.shape, F32), jax.ShapeDtypeStruct(parent_wind.shape, F32)],
            in_specs=[smem, smem] + [vmem] * len(passed),
            out_specs=[anywhere, anywhere],
            scratch_shapes=[
                pltpu.VMEM((ROWS, C, WIDE), F32),
                pltpu.VMEM((ROWS, C, WIDE), F32),
                pltpu.VMEM((PROWS, C, PWIDE), F32),
                pltpu.VMEM((PROWS, C, PWIDE), F32),
                pltpu.VMEM((ROWS, C, 128), F32),
                pltpu.VMEM((ROWS, C, 128), F32),
                pltpu.VMEM((2, C, WIDE), F32),
                pltpu.VMEM((ROWS, 1, 256), F32),
                pltpu.VMEM((256, WIDE), BF16),
                pltpu.SMEM((9, 8, 128), F32),
                pltpu.VMEM((PYD, C, PXD), F32),
                pltpu.VMEM((2 * C * PYD, WIDE), BF16),
                pltpu.SemaphoreType.DMA((9,)),
                pltpu.SemaphoreType.DMA((2 * C,)),
            ],
            compiler_params=pltpu.CompilerParams(vmem_limit_bytes=40 * 2**20),
            name="advance",
        )(diffusion, drift, *rims))

    placed = (
        P(None, "gy", "gx"),
        P(None, "gy", "gx"),
        P(),
        P(),
        P(None, "gy", "gx", None),
        P("gy", "gx", None),
        P("gy", "gx", None),
    )
    return jax.shard_map(
        on_device,
        mesh=mesh,
        in_specs=placed,
        out_specs=(P(None, "gy", "gx"), P(None, "gy", "gx")),
        check_vma=False,
    )
```

```python
import functools

import jax
import jax.numpy as jnp
from jax import lax
from jax.experimental import pallas as pl
from jax.experimental.pallas import tpu as pltpu
from jax.sharding import PartitionSpec as P

C = 16
NYD = 48
NXD = 384
PYD = 16
PXD = 128
MAXD = 8
FOOT = 6
H = 16
PH = 8
NEAR = 6
PNEAR = 2
ROWS = NYD + 2 * H
PROWS = PYD + 2 * PH
WIDE = 512
PWIDE = 256
SLOT = 80
CHUNK = 6
F32 = jnp.float32
BF16 = jnp.bfloat16
MESH = pl.DeviceIdType.MESH
AROUND = ((0, 0), (0, -1), (0, 1), (-1, 0), (1, 0), (-1, -1), (1, -1), (-1, 1), (1, 1))


def lanes_of(shape):
    return lax.broadcasted_iota(jnp.int32, shape, len(shape) - 1)


def turn(value, shift):
    shift = shift % value.shape[-1] if isinstance(shift, int) else shift
    if isinstance(shift, int) and shift == 0:
        return value
    return pltpu.roll(value, shift, value.ndim - 1)


def thrusts(wind, scale):
    half = C // 2
    east, north = wind[:half], wind[half:]
    speed = jnp.sqrt(east * east + north * north + 1.0)
    return scale * wind * jnp.concatenate([speed, speed], axis=0)


def plane_tile(read):
    at = lax.broadcasted_iota(jnp.int32, (C, 128), 0)
    value = jnp.zeros((C, 128), F32)
    for c in range(C):
        value = jnp.where(at == c, read(c), value)
    return value


def factors(spread, east_by, north_by):
    return (1.0 - 4.0 * spread - east_by - north_by, spread + east_by, spread, spread + north_by, spread)


def exchange(tiles_x, tiles_y, nest, parent, diffusion_h, drift_h, sites_h, live_h, coef_h,
             own, south, north, pown, psouth, pnorth, west, east, corner, side, notes,
             pack_w, pack_e, pack_y, own_notes, diffusion, drift, sites, live, coef, in_sem, send_sem, recv_sem):
    gx, gy = lax.axis_index("gx"), lax.axis_index("gy")

    def device(dx, dy):
        return (lax.rem(gx + dx + tiles_x, tiles_x), lax.rem(gy + dy + tiles_y, tiles_y))

    def exists(dx, dy):
        at_x, at_y = gx + dx, gy + dy
        return (at_x >= 0) & (at_x < tiles_x) & (at_y >= 0) & (at_y < tiles_y)

    barrier = pltpu.get_barrier_semaphore()
    around = 0
    for dx, dy in AROUND[1:]:
        around = around + exists(dx, dy).astype(jnp.int32)

        @pl.when(exists(dx, dy))
        def _():
            pl.semaphore_signal(barrier, inc=1, device_id=device(dx, dy), device_id_type=MESH)

    small = ((diffusion_h, diffusion), (drift_h, drift), (sites_h, sites), (live_h, live), (coef_h, coef))
    loads = [pltpu.make_async_copy(nest.at[c], own.at[:, c, :], in_sem.at[c]) for c in range(C)]
    loads += [pltpu.make_async_copy(parent.at[c], pown.at[:, c, :], in_sem.at[C + c]) for c in range(C)]
    loads += [pltpu.make_async_copy(a, b, in_sem.at[2 * C + i]) for i, (a, b) in enumerate(small)]
    for load in loads:
        load.start()
    for load in loads:
        load.wait()

    lane = lanes_of((C, PXD))
    for pack, tile, first in ((pack_w, 0, 0), (pack_e, NXD // 128 - 1, 112)):
        for p in range(NYD // 8):
            packed = jnp.zeros((C, 128), F32)
            for j in range(8):
                cells = own[8 * p + j, :, 128 * tile : 128 * tile + 128]
                packed = jnp.where(lane // 16 == j, turn(cells, 16 * j - first), packed)
            pack[p] = packed
    for way, base in ((0, 0), (1, NYD - H)):
        packed = jnp.zeros((C, 128), F32)
        for i in range(H):
            packed = jnp.where(lane // 4 == i, turn(own[base + i, :, 0:128], 4 * i), packed)
            packed = jnp.where(lane // 4 == H + i, turn(own[base + i, :, NXD - 128 : NXD], 4 * i + 64 - 124), packed)
        pack_y[way] = packed
    strips = []
    edge = jnp.where(gy == tiles_y - 1, PYD - 1, 0)
    after = jnp.where(gy == tiles_y - 1, PYD - 2, 1)
    for first, wide in ((0, 0), (124, 120)):
        packed = jnp.zeros((C, 128), F32)
        for m in range(PYD):
            packed = jnp.where(lane // 4 == PYD + m, turn(pown[m], 64 + 4 * m - first), packed)
        packed = jnp.where(lane // 8 == 6, turn(pown[edge], 48 - wide), packed)
        packed = jnp.where(lane // 8 == 7, turn(pown[after], 56 - wide), packed)
        strips.append(packed)
    shores = []
    for base in (0, PYD - PH):
        packed = jnp.zeros((C, 128), F32)
        for i in range(PH):
            cells = pown[base + i]
            packed = jnp.where(lane // 2 == 24 + i, jnp.where(
                gx == 0, turn(cells, 48 + 2 * i), turn(cells, 48 + 2 * i - 126)), packed)
        shores.append(packed)

    wide_lane = lanes_of((C, NXD))
    inner = (wide_lane >= 4) & (wide_lane < NXD - 4)
    stay, cw, ce, cs, cn = factors(
        plane_tile(lambda c: diffusion[c]), plane_tile(lambda c: drift[0, c]), plane_tile(lambda c: drift[1, c]))
    middle = stay * stay + 2.0 * (cw * ce + cs * cn)

    def three(value):
        return jnp.concatenate([value] * (NXD // 128), axis=1)

    row_weights = [three(v) for v in (cw, stay, ce)]
    square_weights = [three(v) for v in (cw * cw, 2.0 * cw * stay, middle, 2.0 * stay * ce, ce * ce)]
    wind = jnp.zeros((C, PXD), F32)
    scale = jnp.zeros((C, PXD), F32)
    spot = jnp.zeros((C, PXD), F32)
    rests = [jnp.zeros((C, PXD), F32)] * 2

    def total(value):
        return jnp.sum(value, axis=1, keepdims=True)

    for s in range(MAXD):
        row, col = sites[0, 0, 0, s], sites[1, 0, 0, s]
        gap = wide_lane - col
        at_0 = gap == 0
        value = total(jnp.where(at_0, own[row], 0.0))
        wind = jnp.where(lane == s, value, wind)
        push = -(coef[0, 0, s] * live[0, 0, s].astype(F32))
        scale = jnp.where(lane == s, push, scale)
        spot = jnp.where(lane == MAXD + s, row.astype(F32), spot)
        spot = jnp.where(lane == 2 * MAXD + s, col.astype(F32), spot)
        spot = jnp.where(lane == 3 * MAXD + s, push, spot)
        line = jnp.where(gap == -1, row_weights[0], jnp.where(at_0, row_weights[1], jnp.where(gap == 1, row_weights[2], 0.0)))
        square = jnp.zeros((C, NXD), F32)
        for j in range(5):
            square = jnp.where(gap == j - 2, square_weights[j], square)
        near = {r: jnp.where(inner, own[jnp.clip(row + r, 0, NYD - 1)], 0.0) for r in range(-2, 3)}
        along = {r: total(line * near[r]) for r in range(-1, 2)}
        point = {r: total(jnp.where(at_0, near[r], 0.0)) for r in (-2, -1, 1, 2)}
        ones = {0: along[0], -1: cs * point[-1], 1: cn * point[1]}
        twos = {0: total(square * near[0]), -1: 2.0 * cs * along[-1], 1: 2.0 * cn * along[1],
                -2: cs * cs * point[-2], 2: cn * cn * point[2]}
        for way, (low, high) in enumerate(((NEAR, NYD - 1), (0, NYD - 1 - NEAR))):
            for terms, at in ((ones, 4 * MAXD + s), (twos, 5 * MAXD + s)):
                value = jnp.zeros((C, 128), F32)
                for r, term in terms.items():
                    value = value + term * ((row + r >= low) & (row + r <= high)).astype(F32)
                rests[way] = jnp.where(lane == at, value, rests[way])
    mine = thrusts(wind, scale) + spot
    notes[0] = mine
    for i, extra in enumerate((rests[0] + shores[0], rests[1] + shores[1], strips[0], strips[1])):
        own_notes[i] = mine + extra

    for dx, dy, buffers in (
        (0, -1, (south, psouth, side.at[0])), (0, 1, (north, pnorth, side.at[1])), (-1, 0, (west,)), (1, 0, (east,)),
        (-1, -1, (corner.at[0],)), (1, -1, (corner.at[1],)), (-1, 1, (corner.at[2],)), (1, 1, (corner.at[3],)),
    ):
        @pl.when(jnp.logical_not(exists(dx, dy)))
        def _():
            for buffer in buffers + (notes.at[AROUND.index((dx, dy))],):
                buffer[...] = jnp.zeros(buffer.shape, F32)

    sends = [(own_notes.at[0 if dy < 0 else 1] if dx == 0 else own_notes.at[2 if dx < 0 else 3],
              notes.at[AROUND.index((-dx, -dy))], (dx, dy)) for dx, dy in AROUND[:0:-1]]
    sends += [
        (pack_e.at[pl.ds(4, 2)], corner.at[0], (1, 1)),
        (pack_w.at[pl.ds(4, 2)], corner.at[1], (-1, 1)),
        (pack_e.at[pl.ds(0, 2)], corner.at[2], (1, -1)),
        (pack_w.at[pl.ds(0, 2)], corner.at[3], (-1, -1)),
        (pack_e, west, (1, 0)),
        (pack_w, east, (-1, 0)),
        (own.at[pl.ds(NYD - NEAR, NEAR)], south, (0, 1)),
        (own.at[pl.ds(0, NEAR)], north, (0, -1)),
        (pown.at[pl.ds(PYD - PNEAR, PNEAR)], psouth, (0, 1)),
        (pown.at[pl.ds(0, PNEAR)], pnorth, (0, -1)),
        (pack_y.at[1], side.at[0], (0, 1)),
        (pack_y.at[0], side.at[1], (0, -1)),
    ]
    pl.semaphore_wait(barrier, around)
    copies = []
    for i, (source, target, (dx, dy)) in enumerate(sends):
        copy = pltpu.make_async_remote_copy(
            src_ref=source, dst_ref=target, send_sem=send_sem.at[i], recv_sem=recv_sem.at[i],
            device_id=device(dx, dy), device_id_type=MESH,
        )
        copies.append((copy, exists(dx, dy), exists(-dx, -dy)))
        pl.when(exists(dx, dy))(copy.start)
    for copy, sent, received in copies:
        pl.when(sent)(copy.wait_send)
        pl.when(received)(copy.wait_recv)


def advance_all(tiles_x, tiles_y, diffusion, drift, own, south, north, pown, psouth, pnorth, west, east, corner, side, note_in,
                nest_out, parent_out,
                one, two, old, new, cols_old, cols_new, lines, row_g, col_g, places, out_v, sum_v, place_sem, out_sem):
    gx, gy = lax.axis_index("gx"), lax.axis_index("gy")
    lane = lanes_of((C, 128))
    notes = [note_in.at[j] for j in range(9)]
    moves = [pltpu.make_async_copy(note.at[pl.ds(0, 8)], places.at[j], place_sem.at[j]) for j, note in enumerate(notes)]
    for move in moves:
        move.start()

    has_w, has_e = (gx > 0).astype(F32), (gx < tiles_x - 1).astype(F32)
    has_s, has_n = (gy > 0).astype(F32), (gy < tiles_y - 1).astype(F32)
    of_x = {-1: has_w, 0: None, 1: has_e}
    of_y = {-1: has_s, 0: None, 1: has_n}

    push = jnp.zeros((C, 128), F32)
    scale = jnp.zeros((C, 128), F32)
    disk_rows = jnp.full((C, 128), 1.0e6, F32)
    disk_cols = jnp.full((C, 128), 1.0e6, F32)
    missing = [jnp.zeros((C, 128), F32)] * 2
    for j, (dx, dy) in enumerate(AROUND):
        note = notes[j][...]
        here = lane // MAXD == j
        first, force = turn(note, MAXD * j), turn(note, MAXD * j - 3 * MAXD)
        for there in (of_x[dx], of_y[dy]):
            if there is not None:
                first, force = first * there, force * there
        if dx == 0 and dy != 0:
            missing = [jnp.where(here, turn(note, MAXD * j - (4 + i) * MAXD), missing[i]) for i in range(2)]
        push = jnp.where(here, first, push)
        scale = jnp.where(here, force, scale)
        disk_rows = jnp.where(here, turn(note, MAXD * j - MAXD) + float(H + NYD * dy), disk_rows)
        disk_cols = jnp.where(here, turn(note, MAXD * j - 2 * MAXD) + float(NXD * dx), disk_cols)

    def thrice(value):
        shape = value.shape
        at = lanes_of(shape)
        later = turn(value, SLOT)
        return (jnp.where(at < SLOT, value, later),
                jnp.where(at < 2 * SLOT - 128, later, turn(value, 2 * SLOT - 128)))

    def profile(distance):
        return jnp.where(jnp.abs(distance) <= float(FOOT), jnp.exp(distance * distance * (-1.0 / 8.0)), 0.0)

    rows_2 = thrice(disk_rows[0:8])
    height = lax.broadcasted_iota(jnp.int32, (8, 128), 0).astype(F32)
    for block in range(ROWS // 8):
        for half in range(2):
            value = profile(height + float(8 * block) - rows_2[half])
            for j in range(8):
                row_g[8 * block + j, :, 128 * half : 128 * half + 128] = value[j : j + 1]
    cols_2 = thrice(disk_cols[0:8])
    depth_at = lax.broadcasted_iota(jnp.int32, (128, 128), 0)
    for half in range(2):
        across = jnp.transpose(jnp.broadcast_to(cols_2[half][0:1], (128, 128)))
        third = depth_at + 128 * half >= 2 * SLOT
        for tile in range(WIDE // 128):
            at = lanes_of((128, 128)) + 128 * tile
            at = jnp.where(at < 448, at, at - WIDE).astype(F32)
            value = profile(at - across)
            rest = value - value.astype(BF16).astype(F32)
            col_g[128 * half : 128 * half + 128, 128 * tile : 128 * tile + 128] = jnp.where(third, rest, value).astype(BF16)

    def copy_rows(source, base, count):
        def body(i, carry):
            one[base + i, :, 0:NXD] = source[i]
            return carry
        lax.fori_loop(0, count, body, 0)

    copy_rows(south, H - NEAR, NEAR)
    copy_rows(own, H, NYD)
    copy_rows(north, H + NYD, NEAR)
    for p in range(ROWS // 8):
        if p < 2:
            from_w, from_e = corner[0, p], corner[1, p]
        elif p < 8:
            from_w, from_e = west[p - 2], east[p - 2]
        else:
            from_w, from_e = corner[2, p - 8], corner[3, p - 8]
        for j in range(8):
            y = 8 * p + j
            one[y, :, NXD:WIDE] = jnp.where(
                lane < 16, turn(from_e, -16 * j), jnp.where(lane >= 112, turn(from_w, 112 - 16 * j), 0.0))
            if y < H - NEAR or y >= H + NYD + NEAR:
                way, i = (0, y) if y < H else (1, y - H - NYD)
                one[y, :, 0:128] = jnp.where(lane < 4, turn(side[way], -4 * i), 0.0)
                one[y, :, 128 : NXD - 128] = jnp.zeros((C, NXD - 256), F32)
                one[y, :, NXD - 128 : NXD] = jnp.where(lane >= 124, turn(side[way], 60 - 4 * i), 0.0)

    spread = plane_tile(lambda c: diffusion[c])
    east_by = plane_tile(lambda c: drift[0, c])
    north_by = plane_tile(lambda c: drift[1, c])

    def shifted(tiles):
        count = len(tiles)
        up = [turn(v, 1) for v in tiles]
        down = [turn(v, -1) for v in tiles]
        from_w = [jnp.where(lane == 0, up[(t - 1) % count], up[t]) for t in range(count)]
        from_e = [jnp.where(lane == 127, down[(t + 1) % count], down[t]) for t in range(count)]
        return from_w, from_e

    for block, (source, strip_w, strip_e, base, first, count) in enumerate((
        (psouth, note_in[5], note_in[6], 0, PH, PH),
        (pown, note_in[3], note_in[4], PH, 0, PYD),
        (pnorth, note_in[7], note_in[8], PH + PYD, 0, PH),
    )):
        for i in range(count):
            m = first + i
            if block == 0 and i < PH - PNEAR or block == 2 and i >= PNEAR:
                shore = note_in[1 + block // 2]
                middle = jnp.where((lane < 2) & (gx == 0), turn(shore, -48 - 2 * i),
                                   jnp.where((lane >= 126) & (gx == tiles_x - 1), turn(shore, 78 - 2 * i), 0.0))
            else:
                middle = source[i - (PH - PNEAR) if block == 0 else i]
            old[base + i, :, 0:128] = middle
            old[base + i, :, 128:256] = jnp.where(
                lane < 4, turn(strip_e, -64 - 4 * m), jnp.where(lane >= 124, turn(strip_w, 60 - 4 * m), 0.0))

    @pl.when((gy == 0) | (gy == tiles_y - 1))
    def _():
        for i, at in enumerate((jnp.where(gy == 0, PH, PH + PYD - 1), jnp.where(gy == 0, PH + 1, PH + PYD - 2))):
            old[at, :, 128:256] = jnp.where(lane < 8, turn(note_in[4], -48 - 8 * i), jnp.where(
                lane >= 120, turn(note_in[3], 72 - 8 * i), 0.0))

    kept = jnp.where(lane < 64, has_e, has_w)
    stay, cw, ce, cs, cn = factors(spread * (1.0 / 3.0), east_by, north_by)
    new[0] = jnp.zeros((C, PWIDE), F32)
    new[PROWS - 1] = jnp.zeros((C, PWIDE), F32)

    def parent_row(i, carry):
        inside = jnp.where(i < PH, has_s, jnp.where(i >= PH + PYD, has_n, 1.0))
        tiles = [old[i, :, 128 * t : 128 * t + 128] for t in range(2)]
        from_w, from_e = shifted(tiles)
        for t in range(2):
            value = (stay * tiles[t] + cw * from_w[t] + ce * from_e[t]
                     + cs * old[i - 1, :, 128 * t : 128 * t + 128] + cn * old[i + 1, :, 128 * t : 128 * t + 128])
            value = value * inside
            new[i, :, 128 * t : 128 * t + 128] = value * kept if t == 1 else value
        return carry

    lax.fori_loop(1, PROWS - 1, parent_row, 0)

    @pl.when((gx == 0) | (gx == tiles_x - 1))
    def _():
        for source, target in ((old, cols_old), (new, cols_new)):
            for y in range(ROWS):
                q, rest = (y - H) // 3 + PH, (y - H) % 3
                centre = source[q, :, 0:128]
                if rest == 1:
                    value = centre * (2.0 / 3.0)
                else:
                    value = centre * (4.0 / 9.0) + source[q - 1 if rest == 0 else q + 1, :, 0:128] * (2.0 / 9.0)
                target[y] = value

    def pieces(value, count):
        out = []
        for _ in range(count):
            part = value.astype(BF16)
            out.append(part)
            value = value - part.astype(F32)
        return out

    @pl.when((gy == 0) | (gy == tiles_y - 1))
    def _():
        fine = lanes_of((PWIDE, WIDE))
        fine = jnp.where(fine < 448, fine, fine - WIDE)
        coarse = lax.broadcasted_iota(jnp.int32, (PWIDE, WIDE), 0)
        coarse = jnp.where(coarse < 192, coarse, coarse - PWIDE)
        hat = jnp.maximum(3 - jnp.abs(fine - (3 * coarse + 1)), 0).astype(F32).astype(BF16)
        at = jnp.where(gy == 0, PH, PH + PYD - 1)
        parts = pieces(old[at], 3) + pieces(new[at], 3)
        for i in range(2):
            total = jnp.zeros((C, WIDE), F32)
            for part in parts[3 * i : 3 * i + 3]:
                total = total + jnp.dot(part, hat, preferred_element_type=F32)
            lines[i] = total * (2.0 / 9.0)

    stay, cw, ce, cs, cn = factors(spread, east_by, north_by)
    second = [lane + 128 * half for half in range(2)]
    second = [(at >= SLOT) & (at < 2 * SLOT) for at in second]

    def step(source, target, amounts, low, high, k):
        amounts_2 = thrice(amounts)

        def body(i, carry):
            base = low + CHUNK * i
            left = []
            for r in range(CHUNK):
                halves = []
                for half in range(2):
                    value = amounts_2[half] * row_g[base + r, :, 128 * half : 128 * half + 128]
                    rest = value - value.astype(BF16).astype(F32)
                    halves.append(jnp.where(second[half], rest, value).astype(BF16))
                left.append(jnp.concatenate(halves, axis=1))
            force = jnp.dot(jnp.concatenate(left, axis=0), col_g[...], preferred_element_type=F32)
            for r in range(CHUNK):
                y = base + r
                tiles = [source[y, :, 128 * t : 128 * t + 128] for t in range(4)]
                from_w, from_e = shifted(tiles)
                for t in range(4):
                    at = slice(128 * t, 128 * t + 128)
                    target[y, :, at] = (
                        stay * tiles[t] + cw * from_w[t] + ce * from_e[t] + cs * source[y - 1, :, at]
                        + cn * source[y + 1, :, at] + force[C * r : C * r + C, at])
            return carry

        lax.fori_loop(0, (high - low) // CHUNK, body, 0, unroll=True)

        for edge, tile, spot in ((0, 0, 0), (tiles_x - 1, NXD // 128 - 1, 127)):
            @pl.when(gx == edge)
            def _():
                def patch(i, carry):
                    at = slice(128 * tile, 128 * tile + 128)
                    bound = cols_old[i] + (k / 3.0) * (cols_new[i] - cols_old[i])
                    target[i, :, at] = jnp.where(lane == spot, bound, target[i, :, at])
                    return carry
                lax.fori_loop(low, high, patch, 0)
        for edge, row in ((0, H), (tiles_y - 1, H + NYD - 1)):
            @pl.when(gy == edge)
            def _():
                target[row] = lines[0] + (k / 3.0) * (lines[1] - lines[0])

    def gathered(source):
        wind = jnp.zeros((C, 128), F32)
        for j, (dx, dy) in enumerate(AROUND):
            for s in range(MAXD):
                d = MAXD * j + s
                row = places[j, 0, MAXD + s].astype(jnp.int32) + (H + NYD * dy)
                col = places[j, 0, 2 * MAXD + s].astype(jnp.int32) + NXD * dx
                row = jnp.clip(row, 0, ROWS - 1)
                col = jnp.bitwise_and(col, WIDE - 1)
                tile = pl.multiple_of(jnp.bitwise_and(col, WIDE - 128), 128)
                cells = source[row, :, pl.ds(tile, 128)]
                wind = jnp.where(lane == d, turn(cells, jnp.bitwise_and(d - col, 127)), wind)
        return wind

    for buffer, rows in ((two, (0, ROWS - 1)),):
        for row in rows:
            buffer[row] = jnp.zeros((C, WIDE), F32)

    step(one, two, push, 1, ROWS - 1, 1)
    for move in moves:
        move.wait()
    push = thrusts(gathered(two) + missing[0], scale)
    step(two, one, push, 7, ROWS - 7, 2)
    push = thrusts(gathered(one) + missing[1], scale)
    step(one, two, push, 13, ROWS - 13, 3)

    stores = [pltpu.make_async_copy(two.at[pl.ds(H, NYD), c, pl.ds(0, NXD)], nest_out.at[c], out_sem.at[c]) for c in range(C)]
    for store in stores:
        store.start()

    low_side = jnp.where(gx == 0, 0, -64)
    high_side = jnp.where(gx == tiles_x - 1, NXD, NXD + 64)
    fine = lax.broadcasted_iota(jnp.int32, (WIDE, 128), 0)
    fine = jnp.where(fine < 448, fine, fine - WIDE)
    gap = jnp.abs(fine - (3 * lanes_of((WIDE, 128)) + 1))
    weight = jnp.where(gap <= 1, 2.0, jnp.where(gap <= 4, 1.0, 0.0))
    weight = jnp.where((fine >= low_side) & (fine < high_side), weight, 0.0).astype(BF16)

    def three(m):
        y = H + 3 * m
        return two[y] + two[y + 1] + two[y + 2]

    before, here = three(-1) * has_s, three(0)
    high_part, low_part = [], []
    for m in range(PYD):
        after = three(m + 1)
        if m == PYD - 1:
            after = after * has_n
        total = before + 2.0 * here + after
        part = pieces(total, 2)
        sum_v[C * m : C * m + C] = part[0]
        sum_v[C * (PYD + m) : C * (PYD + m) + C] = part[1]
        before, here = here, after
    mean = jnp.dot(sum_v[...], weight, preferred_element_type=F32)
    half = C * PYD
    for m in range(PYD):
        i = m + PH
        tiles = [new[i - 1, :, 128 * t : 128 * t + 128] + 2.0 * new[i, :, 128 * t : 128 * t + 128]
                 + new[i + 1, :, 128 * t : 128 * t + 128] for t in range(2)]
        from_w, from_e = shifted(tiles)
        direct = from_w[0] + 2.0 * tiles[0] + from_e[0]
        out_v[m] = direct * (1.0 / 32.0) + (mean[C * m : C * m + C] + mean[half + C * m : half + C * m + C]) * (1.0 / 288.0)
    last = [pltpu.make_async_copy(out_v.at[:, c, :], parent_out.at[c], out_sem.at[C + c]) for c in range(C)]
    for store in last:
        store.start()
    for store in stores + last:
        store.wait()


def solution(mesh):
    tiles_x, tiles_y = mesh.shape["gx"], mesh.shape["gy"]
    smem = pl.BlockSpec(memory_space=pltpu.SMEM)
    vmem = pl.BlockSpec(memory_space=pltpu.VMEM)
    anywhere = pl.BlockSpec(memory_space=pl.ANY)
    passed = ((NYD, C, NXD), (NEAR, C, NXD), (NEAR, C, NXD), (PYD, C, PXD), (PNEAR, C, PXD), (PNEAR, C, PXD),
              (6, C, 128), (6, C, 128), (4, 2, C, 128), (2, C, 128), (9, C, 128))

    def on_device(nest_wind, parent_wind, diffusion, drift, disk_sites, disk_live, disk_coef):
        rims = pl.pallas_call(
            functools.partial(exchange, tiles_x, tiles_y),
            out_shape=[pltpu.VMEM(shape, F32) for shape in passed],
            in_specs=[pl.BlockSpec(memory_space=pltpu.HBM)] * 7,
            out_specs=[vmem] * len(passed),
            scratch_shapes=[
                pltpu.VMEM((6, C, 128), F32),
                pltpu.VMEM((6, C, 128), F32),
                pltpu.VMEM((2, C, 128), F32),
                pltpu.VMEM((4, C, 128), F32),
                pltpu.SMEM(diffusion.shape, F32),
                pltpu.SMEM(drift.shape, F32),
                pltpu.SMEM((2, 1, 1, MAXD), jnp.int32),
                pltpu.SMEM((1, 1, MAXD), jnp.int32),
                pltpu.SMEM((1, 1, MAXD), F32),
                pltpu.SemaphoreType.DMA((2 * C + 5,)),
                pltpu.SemaphoreType.DMA((20,)),
                pltpu.SemaphoreType.DMA((20,)),
            ],
            compiler_params=pltpu.CompilerParams(
                collective_id=0, has_side_effects=True, vmem_limit_bytes=16 * 2**20),
            name="exchange",
        )(*[pltpu.with_memory_space_constraint(x, pltpu.HBM) for x in
            (nest_wind, parent_wind, diffusion, drift, disk_sites, disk_live, disk_coef)])
        return tuple(pl.pallas_call(
            functools.partial(advance_all, tiles_x, tiles_y),
            out_shape=[jax.ShapeDtypeStruct(nest_wind.shape, F32), jax.ShapeDtypeStruct(parent_wind.shape, F32)],
            in_specs=[smem, smem] + [vmem] * len(passed),
            out_specs=[anywhere, anywhere],
            scratch_shapes=[
                pltpu.VMEM((ROWS, C, WIDE), F32),
                pltpu.VMEM((ROWS, C, WIDE), F32),
                pltpu.VMEM((PROWS, C, PWIDE), F32),
                pltpu.VMEM((PROWS, C, PWIDE), F32),
                pltpu.VMEM((ROWS, C, 128), F32),
                pltpu.VMEM((ROWS, C, 128), F32),
                pltpu.VMEM((2, C, WIDE), F32),
                pltpu.VMEM((ROWS, 1, 256), F32),
                pltpu.VMEM((256, WIDE), BF16),
                pltpu.SMEM((9, 8, 128), F32),
                pltpu.VMEM((PYD, C, PXD), F32),
                pltpu.VMEM((2 * C * PYD, WIDE), BF16),
                pltpu.SemaphoreType.DMA((9,)),
                pltpu.SemaphoreType.DMA((2 * C,)),
            ],
            compiler_params=pltpu.CompilerParams(vmem_limit_bytes=40 * 2**20),
            name="advance",
        )(diffusion, drift, *rims))

    placed = (
        P(None, "gy", "gx"),
        P(None, "gy", "gx"),
        P(),
        P(),
        P(None, "gy", "gx", None),
        P("gy", "gx", None),
        P("gy", "gx", None),
    )
    return jax.shard_map(
        on_device,
        mesh=mesh,
        in_specs=placed,
        out_specs=(P(None, "gy", "gx"), P(None, "gy", "gx")),
        check_vma=False,
    )
```

```python
import functools

import jax
import jax.numpy as jnp
from jax import lax
from jax.experimental import pallas as pl
from jax.experimental.pallas import tpu as pltpu
from jax.sharding import PartitionSpec as P

C = 16
NYD = 48
NXD = 384
PYD = 16
PXD = 128
MAXD = 8
FOOT = 6
H = 16
PH = 8
NEAR = 6
PNEAR = 2
ROWS = NYD + 2 * H
PROWS = PYD + 2 * PH
WIDE = 512
PWIDE = 256
SLOT = 80
CHUNK = 6
F32 = jnp.float32
BF16 = jnp.bfloat16
MESH = pl.DeviceIdType.MESH
AROUND = ((0, 0), (0, -1), (0, 1), (-1, 0), (1, 0), (-1, -1), (1, -1), (-1, 1), (1, 1))


def lanes_of(shape):
    return lax.broadcasted_iota(jnp.int32, shape, len(shape) - 1)


def turn(value, shift):
    shift = shift % value.shape[-1] if isinstance(shift, int) else shift
    if isinstance(shift, int) and shift == 0:
        return value
    return pltpu.roll(value, shift, value.ndim - 1)


def thrusts(wind, scale):
    half = C // 2
    east, north = wind[:half], wind[half:]
    speed = jnp.sqrt(east * east + north * north + 1.0)
    return scale * wind * jnp.concatenate([speed, speed], axis=0)


def plane_tile(read):
    at = lax.broadcasted_iota(jnp.int32, (C, 128), 0)
    value = jnp.zeros((C, 128), F32)
    for c in range(C):
        value = jnp.where(at == c, read(c), value)
    return value


def factors(spread, east_by, north_by):
    return (1.0 - 4.0 * spread - east_by - north_by, spread + east_by, spread, spread + north_by, spread)


def shifted(tiles):
    lane = lanes_of((C, 128))
    count = len(tiles)
    up = [turn(v, 1) for v in tiles]
    down = [turn(v, -1) for v in tiles]
    from_w = [jnp.where(lane == 0, up[(t - 1) % count], up[t]) for t in range(count)]
    from_e = [jnp.where(lane == 127, down[(t + 1) % count], down[t]) for t in range(count)]
    return from_w, from_e


def pieces(value, count):
    out = []
    for _ in range(count):
        part = value.astype(BF16)
        out.append(part)
        value = value - part.astype(F32)
    return out


def thrice(value):
    shape = value.shape
    at = lanes_of(shape)
    later = turn(value, SLOT)
    return (jnp.where(at < SLOT, value, later),
            jnp.where(at < 2 * SLOT - 128, later, turn(value, 2 * SLOT - 128)))


def force_rows(amounts_2, row_g, col_g, base):
    at = lanes_of((C, 128))
    second = (at >= SLOT, at < 2 * SLOT - 128)
    left = []
    for r in range(CHUNK):
        halves = []
        for half in range(2):
            value = amounts_2[half] * row_g[base + r, :, 128 * half : 128 * half + 128]
            rest = value - value.astype(BF16).astype(F32)
            halves.append(jnp.where(second[half], rest, value).astype(BF16))
        left.append(jnp.concatenate(halves, axis=1))
    return jnp.dot(jnp.concatenate(left, axis=0), col_g[...], preferred_element_type=F32)


def exchange(tiles_x, tiles_y, nest, parent, diffusion_h, drift_h, sites_h, live_h, coef_h,
             own, south, north, west, east, corner, side, notes,
             two, new, cols_old, cols_new, lines, row_g, col_g, scale_out, missing_out, weight_out,
             pown, psouth, pnorth, old, pack_w, pack_e, pack_y, own_notes, diffusion, drift, sites, live, coef, in_sem, send_sem, recv_sem):
    gx, gy = lax.axis_index("gx"), lax.axis_index("gy")

    def device(dx, dy):
        return (lax.rem(gx + dx + tiles_x, tiles_x), lax.rem(gy + dy + tiles_y, tiles_y))

    def exists(dx, dy):
        at_x, at_y = gx + dx, gy + dy
        return (at_x >= 0) & (at_x < tiles_x) & (at_y >= 0) & (at_y < tiles_y)

    barrier = pltpu.get_barrier_semaphore()
    around = 0
    for dx, dy in AROUND[1:]:
        around = around + exists(dx, dy).astype(jnp.int32)

        @pl.when(exists(dx, dy))
        def _():
            pl.semaphore_signal(barrier, inc=1, device_id=device(dx, dy), device_id_type=MESH)

    small = ((diffusion_h, diffusion), (drift_h, drift), (sites_h, sites), (live_h, live), (coef_h, coef))
    loads = [pltpu.make_async_copy(nest.at[c], own.at[:, c, :], in_sem.at[c]) for c in range(C)]
    loads += [pltpu.make_async_copy(parent.at[c], pown.at[:, c, :], in_sem.at[C + c]) for c in range(C)]
    loads += [pltpu.make_async_copy(a, b, in_sem.at[2 * C + i]) for i, (a, b) in enumerate(small)]
    for load in loads:
        load.start()
    for load in loads:
        load.wait()

    lane = lanes_of((C, PXD))
    for pack, tile, first in ((pack_w, 0, 0), (pack_e, NXD // 128 - 1, 112)):
        for p in range(NYD // 8):
            packed = jnp.zeros((C, 128), F32)
            for j in range(8):
                cells = own[8 * p + j, :, 128 * tile : 128 * tile + 128]
                packed = jnp.where(lane // 16 == j, turn(cells, 16 * j - first), packed)
            pack[p] = packed
    for way, base in ((0, 0), (1, NYD - H)):
        packed = jnp.zeros((C, 128), F32)
        for i in range(H):
            packed = jnp.where(lane // 4 == i, turn(own[base + i, :, 0:128], 4 * i), packed)
            packed = jnp.where(lane // 4 == H + i, turn(own[base + i, :, NXD - 128 : NXD], 4 * i + 64 - 124), packed)
        pack_y[way] = packed
    strips = []
    edge = jnp.where(gy == tiles_y - 1, PYD - 1, 0)
    after = jnp.where(gy == tiles_y - 1, PYD - 2, 1)
    for first, wide in ((0, 0), (124, 120)):
        packed = jnp.zeros((C, 128), F32)
        for m in range(PYD):
            packed = jnp.where(lane // 4 == PYD + m, turn(pown[m], 64 + 4 * m - first), packed)
        packed = jnp.where(lane // 8 == 6, turn(pown[edge], 48 - wide), packed)
        packed = jnp.where(lane // 8 == 7, turn(pown[after], 56 - wide), packed)
        strips.append(packed)
    shores = []
    for base in (0, PYD - PH):
        packed = jnp.zeros((C, 128), F32)
        for i in range(PH):
            cells = pown[base + i]
            packed = jnp.where(lane // 2 == 24 + i, jnp.where(
                gx == 0, turn(cells, 48 + 2 * i), turn(cells, 48 + 2 * i - 126)), packed)
        shores.append(packed)

    wide_lane = lanes_of((C, NXD))
    inner = (wide_lane >= 4) & (wide_lane < NXD - 4)
    spread = plane_tile(lambda c: diffusion[c])
    east_by = plane_tile(lambda c: drift[0, c])
    north_by = plane_tile(lambda c: drift[1, c])
    stay, cw, ce, cs, cn = factors(
        spread, east_by, north_by)
    middle = stay * stay + 2.0 * (cw * ce + cs * cn)

    def three(value):
        return jnp.concatenate([value] * (NXD // 128), axis=1)

    row_weights = [three(v) for v in (cw, stay, ce)]
    square_weights = [three(v) for v in (cw * cw, 2.0 * cw * stay, middle, 2.0 * stay * ce, ce * ce)]
    wind = jnp.zeros((C, PXD), F32)
    scale = jnp.zeros((C, PXD), F32)
    spot = jnp.zeros((C, PXD), F32)
    rests = [jnp.zeros((C, PXD), F32)] * 2

    def total(value):
        return jnp.sum(value, axis=1, keepdims=True)

    for s in range(MAXD):
        row, col = sites[0, 0, 0, s], sites[1, 0, 0, s]
        gap = wide_lane - col
        at_0 = gap == 0
        value = total(jnp.where(at_0, own[row], 0.0))
        wind = jnp.where(lane == s, value, wind)
        push = -(coef[0, 0, s] * live[0, 0, s].astype(F32))
        scale = jnp.where(lane == s, push, scale)
        spot = jnp.where(lane == MAXD + s, row.astype(F32), spot)
        spot = jnp.where(lane == 2 * MAXD + s, col.astype(F32), spot)
        spot = jnp.where(lane == 3 * MAXD + s, push, spot)
        line = jnp.where(gap == -1, row_weights[0], jnp.where(at_0, row_weights[1], jnp.where(gap == 1, row_weights[2], 0.0)))
        square = jnp.zeros((C, NXD), F32)
        for j in range(5):
            square = jnp.where(gap == j - 2, square_weights[j], square)
        near = {r: jnp.where(inner, own[jnp.clip(row + r, 0, NYD - 1)], 0.0) for r in range(-2, 3)}
        along = {r: total(line * near[r]) for r in range(-1, 2)}
        point = {r: total(jnp.where(at_0, near[r], 0.0)) for r in (-2, -1, 1, 2)}
        ones = {0: along[0], -1: cs * point[-1], 1: cn * point[1]}
        twos = {0: total(square * near[0]), -1: 2.0 * cs * along[-1], 1: 2.0 * cn * along[1],
                -2: cs * cs * point[-2], 2: cn * cn * point[2]}
        for way, (low, high) in enumerate(((NEAR, NYD - 1), (0, NYD - 1 - NEAR))):
            for terms, at in ((ones, 4 * MAXD + s), (twos, 5 * MAXD + s)):
                value = jnp.zeros((C, 128), F32)
                for r, term in terms.items():
                    value = value + term * ((row + r >= low) & (row + r <= high)).astype(F32)
                rests[way] = jnp.where(lane == at, value, rests[way])
    mine = thrusts(wind, scale) + spot
    notes[0] = mine
    for i, extra in enumerate((rests[0] + shores[0], rests[1] + shores[1], strips[0], strips[1])):
        own_notes[i] = mine + extra

    for dx, dy, buffers in (
        (0, -1, (south, psouth, side.at[0])), (0, 1, (north, pnorth, side.at[1])), (-1, 0, (west,)), (1, 0, (east,)),
        (-1, -1, (corner.at[0],)), (1, -1, (corner.at[1],)), (-1, 1, (corner.at[2],)), (1, 1, (corner.at[3],)),
    ):
        @pl.when(jnp.logical_not(exists(dx, dy)))
        def _():
            for buffer in buffers + (notes.at[AROUND.index((dx, dy))],):
                buffer[...] = jnp.zeros(buffer.shape, F32)

    sends = [(own_notes.at[0 if dy < 0 else 1] if dx == 0 else own_notes.at[2 if dx < 0 else 3],
              notes.at[AROUND.index((-dx, -dy))], (dx, dy)) for dx, dy in AROUND[:0:-1]]
    sends += [
        (pown.at[pl.ds(PYD - PNEAR, PNEAR)], psouth, (0, 1)),
        (pown.at[pl.ds(0, PNEAR)], pnorth, (0, -1)),
        (pack_e.at[pl.ds(4, 2)], corner.at[0], (1, 1)),
        (pack_w.at[pl.ds(4, 2)], corner.at[1], (-1, 1)),
        (pack_e.at[pl.ds(0, 2)], corner.at[2], (1, -1)),
        (pack_w.at[pl.ds(0, 2)], corner.at[3], (-1, -1)),
        (pack_e, west, (1, 0)),
        (pack_w, east, (-1, 0)),
        (own.at[pl.ds(NYD - NEAR, NEAR)], south, (0, 1)),
        (own.at[pl.ds(0, NEAR)], north, (0, -1)),
        (pack_y.at[1], side.at[0], (0, 1)),
        (pack_y.at[0], side.at[1], (0, -1)),
    ]
    pl.semaphore_wait(barrier, around)
    copies = []
    for i, (source, target, (dx, dy)) in enumerate(sends):
        copy = pltpu.make_async_remote_copy(
            src_ref=source, dst_ref=target, send_sem=send_sem.at[i], recv_sem=recv_sem.at[i],
            device_id=device(dx, dy), device_id_type=MESH,
        )
        copies.append((copy, exists(dx, dy), exists(-dx, -dy)))
        pl.when(exists(dx, dy))(copy.start)
    def own_row(i, carry):
        tiles = [own[i, :, 128 * t : 128 * t + 128] for t in range(3)]
        up = [turn(v, 1) for v in tiles]
        down = [turn(v, -1) for v in tiles]
        below, above = own[jnp.maximum(i - 1, 0)], own[jnp.minimum(i + 1, NYD - 1)]
        below_by = cs * (i > 0).astype(F32)
        above_by = cn * (i < NYD - 1).astype(F32)
        for t in range(3):
            from_w = jnp.where(lane == 0, up[t - 1] if t > 0 else 0.0, up[t])
            from_e = jnp.where(lane == 127, down[t + 1] if t < 2 else 0.0, down[t])
            at = slice(128 * t, 128 * t + 128)
            two[H + i, :, at] = (stay * tiles[t] + cw * from_w + ce * from_e
                                 + below_by * below[:, at] + above_by * above[:, at])
        two[H + i, :, NXD:WIDE] = jnp.where(lane == 0, cw * up[2], jnp.where(lane == 127, ce * down[0], 0.0))
        return carry

    lax.fori_loop(0, NYD, own_row, 0, unroll=4)

    def clear(i, carry):
        two[i] = jnp.zeros((C, WIDE), F32)
        two[H + NYD + i] = jnp.zeros((C, WIDE), F32)
        return carry

    lax.fori_loop(0, H, clear, 0)

    early = len(AROUND) + 1
    for copy, sent, received in copies[:early]:
        pl.when(received)(copy.wait_recv)
    has_w, has_e = (gx > 0).astype(F32), (gx < tiles_x - 1).astype(F32)
    has_s, has_n = (gy > 0).astype(F32), (gy < tiles_y - 1).astype(F32)
    of_x = {-1: has_w, 0: None, 1: has_e}
    of_y = {-1: has_s, 0: None, 1: has_n}

    push = jnp.zeros((C, 128), F32)
    scale = jnp.zeros((C, 128), F32)
    disk_rows = jnp.full((C, 128), 1.0e6, F32)
    disk_cols = jnp.full((C, 128), 1.0e6, F32)
    missing = [jnp.zeros((C, 128), F32)] * 2
    for j, (dx, dy) in enumerate(AROUND):
        note = notes[j]
        here = lane // MAXD == j
        first, force = turn(note, MAXD * j), turn(note, MAXD * j - 3 * MAXD)
        for there in (of_x[dx], of_y[dy]):
            if there is not None:
                first, force = first * there, force * there
        if dx == 0 and dy != 0:
            missing = [jnp.where(here, turn(note, MAXD * j - (4 + i) * MAXD), missing[i]) for i in range(2)]
        push = jnp.where(here, first, push)
        scale = jnp.where(here, force, scale)
        disk_rows = jnp.where(here, turn(note, MAXD * j - MAXD) + float(H + NYD * dy), disk_rows)
        disk_cols = jnp.where(here, turn(note, MAXD * j - 2 * MAXD) + float(NXD * dx), disk_cols)

    def profile(distance):
        return jnp.where(jnp.abs(distance) <= float(FOOT), jnp.exp(distance * distance * (-1.0 / 8.0)), 0.0)

    rows_2 = thrice(disk_rows[0:8])
    height = lax.broadcasted_iota(jnp.int32, (8, 128), 0).astype(F32)
    for block in range(ROWS // 8):
        for half in range(2):
            value = profile(height + float(8 * block) - rows_2[half])
            for j in range(8):
                row_g[8 * block + j, :, 128 * half : 128 * half + 128] = value[j : j + 1]
    cols_2 = thrice(disk_cols[0:8])
    depth_at = lax.broadcasted_iota(jnp.int32, (128, 128), 0)
    for half in range(2):
        across = jnp.transpose(jnp.broadcast_to(cols_2[half][0:1], (128, 128)))
        third = depth_at + 128 * half >= 2 * SLOT
        for tile in range(WIDE // 128):
            at = lanes_of((128, 128)) + 128 * tile
            at = jnp.where(at < 448, at, at - WIDE).astype(F32)
            value = profile(at - across)
            rest = value - value.astype(BF16).astype(F32)
            col_g[128 * half : 128 * half + 128, 128 * tile : 128 * tile + 128] = jnp.where(third, rest, value).astype(BF16)
    scale_out[...] = scale
    for i in range(2):
        missing_out[i] = missing[i]

    low_side = jnp.where(gx == 0, 0, -64)
    high_side = jnp.where(gx == tiles_x - 1, NXD, NXD + 64)
    fine = lax.broadcasted_iota(jnp.int32, (WIDE, 128), 0)
    fine = jnp.where(fine < 448, fine, fine - WIDE)
    gap = jnp.abs(fine - (3 * lanes_of((WIDE, 128)) + 1))
    weight = jnp.where(gap <= 1, 2.0, jnp.where(gap <= 4, 1.0, 0.0))
    weight_out[...] = jnp.where((fine >= low_side) & (fine < high_side), weight, 0.0).astype(BF16)

    for block, (source, strip_w, strip_e, base, first, count) in enumerate((
        (psouth, notes[5], notes[6], 0, PH, PH),
        (pown, notes[3], notes[4], PH, 0, PYD),
        (pnorth, notes[7], notes[8], PH + PYD, 0, PH),
    )):
        for i in range(count):
            m = first + i
            if block == 0 and i < PH - PNEAR or block == 2 and i >= PNEAR:
                shore = notes[1 + block // 2]
                middle = jnp.where((lane < 2) & (gx == 0), turn(shore, -48 - 2 * i),
                                   jnp.where((lane >= 126) & (gx == tiles_x - 1), turn(shore, 78 - 2 * i), 0.0))
            else:
                middle = source[i - (PH - PNEAR) if block == 0 else i]
            old[base + i, :, 0:128] = middle
            old[base + i, :, 128:256] = jnp.where(
                lane < 4, turn(strip_e, -64 - 4 * m), jnp.where(lane >= 124, turn(strip_w, 60 - 4 * m), 0.0))

    @pl.when((gy == 0) | (gy == tiles_y - 1))
    def _():
        for i, at in enumerate((jnp.where(gy == 0, PH, PH + PYD - 1), jnp.where(gy == 0, PH + 1, PH + PYD - 2))):
            old[at, :, 128:256] = jnp.where(lane < 8, turn(notes[4], -48 - 8 * i), jnp.where(
                lane >= 120, turn(notes[3], 72 - 8 * i), 0.0))

    kept = jnp.where(lane < 64, has_e, has_w)
    stay, cw, ce, cs, cn = factors(spread * (1.0 / 3.0), east_by, north_by)
    new[0] = jnp.zeros((C, PWIDE), F32)
    new[PROWS - 1] = jnp.zeros((C, PWIDE), F32)

    def parent_row(i, carry):
        inside = jnp.where(i < PH, has_s, jnp.where(i >= PH + PYD, has_n, 1.0))
        tiles = [old[i, :, 128 * t : 128 * t + 128] for t in range(2)]
        from_w, from_e = shifted(tiles)
        for t in range(2):
            value = (stay * tiles[t] + cw * from_w[t] + ce * from_e[t]
                     + cs * old[i - 1, :, 128 * t : 128 * t + 128] + cn * old[i + 1, :, 128 * t : 128 * t + 128])
            value = value * inside
            new[i, :, 128 * t : 128 * t + 128] = value * kept if t == 1 else value
        return carry

    lax.fori_loop(1, PROWS - 1, parent_row, 0)

    @pl.when((gx == 0) | (gx == tiles_x - 1))
    def _():
        for source, target in ((old, cols_old), (new, cols_new)):
            for y in range(ROWS):
                q, rest = (y - H) // 3 + PH, (y - H) % 3
                centre = source[q, :, 0:128]
                if rest == 1:
                    value = centre * (2.0 / 3.0)
                else:
                    value = centre * (4.0 / 9.0) + source[q - 1 if rest == 0 else q + 1, :, 0:128] * (2.0 / 9.0)
                target[y] = value

    @pl.when((gy == 0) | (gy == tiles_y - 1))
    def _():
        fine = lanes_of((PWIDE, WIDE))
        fine = jnp.where(fine < 448, fine, fine - WIDE)
        coarse = lax.broadcasted_iota(jnp.int32, (PWIDE, WIDE), 0)
        coarse = jnp.where(coarse < 192, coarse, coarse - PWIDE)
        hat = jnp.maximum(3 - jnp.abs(fine - (3 * coarse + 1)), 0).astype(F32).astype(BF16)
        at = jnp.where(gy == 0, PH, PH + PYD - 1)
        parts = pieces(old[at], 3) + pieces(new[at], 3)
        for i in range(2):
            total = jnp.zeros((C, WIDE), F32)
            for part in parts[3 * i : 3 * i + 3]:
                total = total + jnp.dot(part, hat, preferred_element_type=F32)
            lines[i] = total * (2.0 / 9.0)

    amounts_2 = thrice(push)

    def first_force(i, carry):
        base = 1 + CHUNK * i
        force = force_rows(amounts_2, row_g, col_g, base)
        for r in range(CHUNK):
            two[base + r] += force[C * r : C * r + C]
        return carry

    lax.fori_loop(0, (ROWS - 2) // CHUNK, first_force, 0)

    for i, (copy, sent, received) in enumerate(copies):
        pl.when(sent)(copy.wait_send)
        if i >= early:
            pl.when(received)(copy.wait_recv)


def advance_all(tiles_x, tiles_y, diffusion, drift, own, south, north, west, east, corner, side, note_in,
                begun, new, cols_old, cols_new, lines, row_g, col_g, scale_in, missing, weight_in,
                nest_out, parent_out,
                one, two, places, out_v, sum_v, place_sem, out_sem):
    gx, gy = lax.axis_index("gx"), lax.axis_index("gy")
    lane = lanes_of((C, 128))
    notes = [note_in.at[j] for j in range(9)]
    moves = [pltpu.make_async_copy(note.at[pl.ds(0, 8)], places.at[j], place_sem.at[j]) for j, note in enumerate(notes)]
    for move in moves:
        move.start()
    has_s, has_n = (gy > 0).astype(F32), (gy < tiles_y - 1).astype(F32)
    scale = scale_in[...]

    def copy_rows(source, base, count):
        def body(i, carry):
            one[base + i, :, 0:NXD] = source[i]
            return carry
        lax.fori_loop(0, count, body, 0)

    copy_rows(south, H - NEAR, NEAR)
    one[H, :, 0:NXD] = own[0]
    one[H + NYD - 1, :, 0:NXD] = own[NYD - 1]
    copy_rows(north, H + NYD, NEAR)
    for p in range(ROWS // 8):
        if p < 2:
            from_w, from_e = corner[0, p], corner[1, p]
        elif p < 8:
            from_w, from_e = west[p - 2], east[p - 2]
        else:
            from_w, from_e = corner[2, p - 8], corner[3, p - 8]
        for j in range(8):
            y = 8 * p + j
            one[y, :, NXD:WIDE] = jnp.where(
                lane < 16, turn(from_e, -16 * j), jnp.where(lane >= 112, turn(from_w, 112 - 16 * j), 0.0))
            if y < H - NEAR or y >= H + NYD + NEAR:
                way, i = (0, y) if y < H else (1, y - H - NYD)
                one[y, :, 0:128] = jnp.where(lane < 4, turn(side[way], -4 * i), 0.0)
                one[y, :, 128 : NXD - 128] = jnp.zeros((C, NXD - 256), F32)
                one[y, :, NXD - 128 : NXD] = jnp.where(lane >= 124, turn(side[way], 60 - 4 * i), 0.0)

    spread = plane_tile(lambda c: diffusion[c])
    east_by = plane_tile(lambda c: drift[0, c])
    north_by = plane_tile(lambda c: drift[1, c])

    stay, cw, ce, cs, cn = factors(spread, east_by, north_by)
    def swept(source, y):
        tiles = [source[y, :, 128 * t : 128 * t + 128] for t in range(4)]
        from_w, from_e = shifted(tiles)
        out = []
        for t in range(4):
            at = slice(128 * t, 128 * t + 128)
            out.append(stay * tiles[t] + cw * from_w[t] + ce * from_e[t]
                       + cs * source[y - 1, :, at] + cn * source[y + 1, :, at])
        return out

    def finish_first():
        def frame(i, carry):
            for y in (1 + i, H + NYD + i):
                for t, value in enumerate(swept(one, y)):
                    at = slice(128 * t, 128 * t + 128)
                    two[y, :, at] = begun[y, :, at] + value
            return carry

        lax.fori_loop(0, H - 1, frame, 0, unroll=3)

        def inside(i, carry):
            y = H + i
            tile = one[y, :, NXD:WIDE]
            up, down = turn(tile, 1), turn(tile, -1)
            two[y, :, 0:128] = begun[y, :, 0:128] + jnp.where(lane == 0, cw * up, 0.0)
            two[y, :, 128:256] = begun[y, :, 128:256]
            two[y, :, 256:384] = begun[y, :, 256:384] + jnp.where(lane == 127, ce * down, 0.0)
            two[y, :, NXD:WIDE] = (
                begun[y, :, NXD:WIDE] + stay * tile + jnp.where(lane == 0, 0.0, cw * up)
                + jnp.where(lane == 127, 0.0, ce * down) + cs * one[y - 1, :, NXD:WIDE] + cn * one[y + 1, :, NXD:WIDE])
            return carry

        lax.fori_loop(0, NYD, inside, 0, unroll=6)
        for y, by, beyond in ((H, cs, H - 1), (H + NYD - 1, cn, H + NYD)):
            for t in range(3):
                at = slice(128 * t, 128 * t + 128)
                two[y, :, at] += by * one[beyond, :, at]
        hold_edges(two, 1, ROWS - 1, 1)

    def hold_edges(target, low, high, k):
        for edge, tile, spot in ((0, 0, 0), (tiles_x - 1, NXD // 128 - 1, 127)):
            @pl.when(gx == edge)
            def _():
                def patch(i, carry):
                    at = slice(128 * tile, 128 * tile + 128)
                    bound = cols_old[i] + (k / 3.0) * (cols_new[i] - cols_old[i])
                    target[i, :, at] = jnp.where(lane == spot, bound, target[i, :, at])
                    return carry
                lax.fori_loop(low, high, patch, 0, unroll=6)
        for edge, row in ((0, H), (tiles_y - 1, H + NYD - 1)):
            @pl.when(gy == edge)
            def _():
                target[row] = lines[0] + (k / 3.0) * (lines[1] - lines[0])

    def step(source, target, amounts, low, high, k):
        amounts_2 = thrice(amounts)

        def body(i, carry):
            base = low + CHUNK * i
            force = force_rows(amounts_2, row_g, col_g, base)
            for r in range(CHUNK):
                for t, value in enumerate(swept(source, base + r)):
                    at = slice(128 * t, 128 * t + 128)
                    target[base + r, :, at] = value + force[C * r : C * r + C, at]
            return carry

        lax.fori_loop(0, (high - low) // CHUNK, body, 0, unroll=True)
        hold_edges(target, low, high, k)

    def gathered(source):
        wind = jnp.zeros((C, 128), F32)
        for j, (dx, dy) in enumerate(AROUND):
            for s in range(MAXD):
                d = MAXD * j + s
                row = places[j, 0, MAXD + s].astype(jnp.int32) + (H + NYD * dy)
                col = places[j, 0, 2 * MAXD + s].astype(jnp.int32) + NXD * dx
                row = jnp.clip(row, 0, ROWS - 1)
                col = jnp.bitwise_and(col, WIDE - 1)
                tile = pl.multiple_of(jnp.bitwise_and(col, WIDE - 128), 128)
                cells = source[row, :, pl.ds(tile, 128)]
                wind = jnp.where(lane == d, turn(cells, jnp.bitwise_and(d - col, 127)), wind)
        return wind

    for buffer, rows in ((two, (0, ROWS - 1)),):
        for row in rows:
            buffer[row] = jnp.zeros((C, WIDE), F32)

    finish_first()
    for move in moves:
        move.wait()
    push = thrusts(gathered(two) + missing[0], scale)
    step(two, one, push, 7, ROWS - 7, 2)
    push = thrusts(gathered(one) + missing[1], scale)
    step(one, two, push, 13, ROWS - 13, 3)

    stores = [pltpu.make_async_copy(two.at[pl.ds(H, NYD), c, pl.ds(0, NXD)], nest_out.at[c], out_sem.at[c]) for c in range(C)]
    for store in stores:
        store.start()

    def three(m):
        y = H + 3 * m
        return two[y] + two[y + 1] + two[y + 2]

    before, here = three(-1) * has_s, three(0)
    high_part, low_part = [], []
    for m in range(PYD):
        after = three(m + 1)
        if m == PYD - 1:
            after = after * has_n
        total = before + 2.0 * here + after
        part = pieces(total, 2)
        sum_v[C * m : C * m + C] = part[0]
        sum_v[C * (PYD + m) : C * (PYD + m) + C] = part[1]
        before, here = here, after
    mean = jnp.dot(sum_v[...], weight_in[...], preferred_element_type=F32)
    half = C * PYD
    for m in range(PYD):
        i = m + PH
        tiles = [new[i - 1, :, 128 * t : 128 * t + 128] + 2.0 * new[i, :, 128 * t : 128 * t + 128]
                 + new[i + 1, :, 128 * t : 128 * t + 128] for t in range(2)]
        from_w, from_e = shifted(tiles)
        direct = from_w[0] + 2.0 * tiles[0] + from_e[0]
        out_v[m] = direct * (1.0 / 32.0) + (mean[C * m : C * m + C] + mean[half + C * m : half + C * m + C]) * (1.0 / 288.0)
    last = [pltpu.make_async_copy(out_v.at[:, c, :], parent_out.at[c], out_sem.at[C + c]) for c in range(C)]
    for store in last:
        store.start()
    for store in stores + last:
        store.wait()


def solution(mesh):
    tiles_x, tiles_y = mesh.shape["gx"], mesh.shape["gy"]
    smem = pl.BlockSpec(memory_space=pltpu.SMEM)
    vmem = pl.BlockSpec(memory_space=pltpu.VMEM)
    anywhere = pl.BlockSpec(memory_space=pl.ANY)
    passed = ((NYD, C, NXD), (NEAR, C, NXD), (NEAR, C, NXD),
              (6, C, 128), (6, C, 128), (4, 2, C, 128), (2, C, 128), (9, C, 128),
              (ROWS, C, WIDE), (PROWS, C, PWIDE), (ROWS, C, 128), (ROWS, C, 128), (2, C, WIDE), (ROWS, 1, 256),
              (256, WIDE), (C, 128), (2, C, 128), (WIDE, 128))
    halved = (14, 17)

    def on_device(nest_wind, parent_wind, diffusion, drift, disk_sites, disk_live, disk_coef):
        rims = pl.pallas_call(
            functools.partial(exchange, tiles_x, tiles_y),
            out_shape=[pltpu.VMEM(shape, BF16 if i in halved else F32) for i, shape in enumerate(passed)],
            in_specs=[pl.BlockSpec(memory_space=pltpu.HBM)] * 7,
            out_specs=[vmem] * len(passed),
            scratch_shapes=[
                pltpu.VMEM((PYD, C, PXD), F32),
                pltpu.VMEM((PNEAR, C, PXD), F32),
                pltpu.VMEM((PNEAR, C, PXD), F32),
                pltpu.VMEM((PROWS, C, PWIDE), F32),
                pltpu.VMEM((6, C, 128), F32),
                pltpu.VMEM((6, C, 128), F32),
                pltpu.VMEM((2, C, 128), F32),
                pltpu.VMEM((4, C, 128), F32),
                pltpu.SMEM(diffusion.shape, F32),
                pltpu.SMEM(drift.shape, F32),
                pltpu.SMEM((2, 1, 1, MAXD), jnp.int32),
                pltpu.SMEM((1, 1, MAXD), jnp.int32),
                pltpu.SMEM((1, 1, MAXD), F32),
                pltpu.SemaphoreType.DMA((2 * C + 5,)),
                pltpu.SemaphoreType.DMA((20,)),
                pltpu.SemaphoreType.DMA((20,)),
            ],
            compiler_params=pltpu.CompilerParams(
                collective_id=0, has_side_effects=True, vmem_limit_bytes=16 * 2**20),
            name="exchange",
        )(*[pltpu.with_memory_space_constraint(x, pltpu.HBM) for x in
            (nest_wind, parent_wind, diffusion, drift, disk_sites, disk_live, disk_coef)])
        return tuple(pl.pallas_call(
            functools.partial(advance_all, tiles_x, tiles_y),
            out_shape=[jax.ShapeDtypeStruct(nest_wind.shape, F32), jax.ShapeDtypeStruct(parent_wind.shape, F32)],
            in_specs=[smem, smem] + [vmem] * len(passed),
            out_specs=[anywhere, anywhere],
            scratch_shapes=[
                pltpu.VMEM((ROWS, C, WIDE), F32),
                pltpu.VMEM((ROWS, C, WIDE), F32),
                pltpu.SMEM((9, 8, 128), F32),
                pltpu.VMEM((PYD, C, PXD), F32),
                pltpu.VMEM((2 * C * PYD, WIDE), BF16),
                pltpu.SemaphoreType.DMA((9,)),
                pltpu.SemaphoreType.DMA((2 * C,)),
            ],
            compiler_params=pltpu.CompilerParams(vmem_limit_bytes=40 * 2**20),
            name="advance",
        )(diffusion, drift, *rims))

    placed = (
        P(None, "gy", "gx"),
        P(None, "gy", "gx"),
        P(),
        P(),
        P(None, "gy", "gx", None),
        P("gy", "gx", None),
        P("gy", "gx", None),
    )
    return jax.shard_map(
        on_device,
        mesh=mesh,
        in_specs=placed,
        out_specs=(P(None, "gy", "gx"), P(None, "gy", "gx")),
        check_vma=False,
    )
```

```python
import functools

import jax
import jax.numpy as jnp
from jax import lax
from jax.experimental import pallas as pl
from jax.experimental.pallas import tpu as pltpu
from jax.sharding import PartitionSpec as P

C = 16
NYD = 48
NXD = 384
PYD = 16
PXD = 128
MAXD = 8
FOOT = 6
H = 16
PH = 8
NEAR = 6
PNEAR = 2
NARROW = 8
RIM = (0, 1, NYD - 2, NYD - 1)
ROWS = NYD + 2 * H
PROWS = PYD + 2 * PH
WIDE = 512
PWIDE = 256
SLOT = 80
CHUNK = 6
F32 = jnp.float32
BF16 = jnp.bfloat16
MESH = pl.DeviceIdType.MESH
AROUND = ((0, 0), (0, -1), (0, 1), (-1, 0), (1, 0), (-1, -1), (1, -1), (-1, 1), (1, 1))


def lanes_of(shape):
    return lax.broadcasted_iota(jnp.int32, shape, len(shape) - 1)


def turn(value, shift):
    shift = shift % value.shape[-1] if isinstance(shift, int) else shift
    if isinstance(shift, int) and shift == 0:
        return value
    return pltpu.roll(value, shift, value.ndim - 1)


def thrusts(wind, scale):
    half = C // 2
    east, north = wind[:half], wind[half:]
    speed = jnp.sqrt(east * east + north * north + 1.0)
    return scale * wind * jnp.concatenate([speed, speed], axis=0)


def plane_tile(read):
    at = lax.broadcasted_iota(jnp.int32, (C, 128), 0)
    value = jnp.zeros((C, 128), F32)
    for c in range(C):
        value = jnp.where(at == c, read(c), value)
    return value


def factors(spread, east_by, north_by):
    return (1.0 - 4.0 * spread - east_by - north_by, spread + east_by, spread, spread + north_by, spread)


def shifted(tiles):
    lane = lanes_of((C, 128))
    count = len(tiles)
    up = [turn(v, 1) for v in tiles]
    down = [turn(v, -1) for v in tiles]
    from_w = [jnp.where(lane == 0, up[(t - 1) % count], up[t]) for t in range(count)]
    from_e = [jnp.where(lane == 127, down[(t + 1) % count], down[t]) for t in range(count)]
    return from_w, from_e


def pieces(value, count):
    out = []
    for _ in range(count):
        part = value.astype(BF16)
        out.append(part)
        value = value - part.astype(F32)
    return out


def thrice(value):
    shape = value.shape
    at = lanes_of(shape)
    later = turn(value, SLOT)
    return (jnp.where(at < SLOT, value, later),
            jnp.where(at < 2 * SLOT - 128, later, turn(value, 2 * SLOT - 128)))


def force_rows(amounts_2, row_g, col_g, base):
    at = lanes_of((C, 128))
    second = (at >= SLOT, at < 2 * SLOT - 128)
    left = []
    for r in range(CHUNK):
        halves = []
        for half in range(2):
            value = amounts_2[half] * row_g[base + r, :, 128 * half : 128 * half + 128]
            rest = value - value.astype(BF16).astype(F32)
            halves.append(jnp.where(second[half], rest, value).astype(BF16))
        left.append(jnp.concatenate(halves, axis=1))
    return jnp.dot(jnp.concatenate(left, axis=0), col_g[...], preferred_element_type=F32)


def exchange(tiles_x, tiles_y, nest, parent, diffusion_h, drift_h, sites_h, live_h, coef_h,
             own, south, north, west, east, corner, side, notes,
             two, new, cols_old, cols_new, lines, row_g, col_g, scale_out, missing_out, weight_out,
             pown, psouth, pnorth, old, strip_w, strip_e, pack_w, pack_e, pack_y, own_notes, diffusion, drift, sites, live, coef, in_sem, send_sem, recv_sem):
    gx, gy = lax.axis_index("gx"), lax.axis_index("gy")

    def device(dx, dy):
        return (lax.rem(gx + dx + tiles_x, tiles_x), lax.rem(gy + dy + tiles_y, tiles_y))

    def exists(dx, dy):
        at_x, at_y = gx + dx, gy + dy
        return (at_x >= 0) & (at_x < tiles_x) & (at_y >= 0) & (at_y < tiles_y)

    barrier = pltpu.get_barrier_semaphore()
    around = 0
    for dx, dy in AROUND[1:]:
        around = around + exists(dx, dy).astype(jnp.int32)

        @pl.when(exists(dx, dy))
        def _():
            pl.semaphore_signal(barrier, inc=1, device_id=device(dx, dy), device_id_type=MESH)

    small = ((diffusion_h, diffusion), (drift_h, drift), (sites_h, sites), (live_h, live), (coef_h, coef))
    loads = [pltpu.make_async_copy(nest.at[c], own.at[:, c, :], in_sem.at[c]) for c in range(C)]
    loads += [pltpu.make_async_copy(parent.at[c], pown.at[:, c, :], in_sem.at[C + c]) for c in range(C)]
    loads += [pltpu.make_async_copy(a, b, in_sem.at[2 * C + i]) for i, (a, b) in enumerate(small)]
    for load in loads:
        load.start()
    for load in loads:
        load.wait()

    lane = lanes_of((C, PXD))
    for pack, tile, first in ((pack_w, 0, 0), (pack_e, NXD // 128 - 1, 112)):
        for i, p in enumerate((0, 1, 4, 5)):
            packed = jnp.zeros((C, 128), F32)
            for j in range(8):
                cells = own[8 * p + j, :, 128 * tile : 128 * tile + 128]
                packed = jnp.where(lane // 16 == j, turn(cells, 16 * j - first), packed)
            pack[i] = packed
    for strip, tile, first in ((strip_w, 0, 0), (strip_e, NXD // 128 - 1, 120)):
        for p in range(NYD // 16):
            packed = jnp.zeros((C, 128), F32)
            for j in range(16):
                cells = own[16 * p + j, :, 128 * tile : 128 * tile + 128]
                packed = jnp.where(lane // 8 == j, turn(cells, 8 * j - first), packed)
            strip[p] = packed
    for way, base in ((0, 0), (1, NYD - H)):
        packed = jnp.zeros((C, 128), F32)
        for i in range(H):
            packed = jnp.where(lane // 4 == i, turn(own[base + i, :, 0:128], 4 * i), packed)
            packed = jnp.where(lane // 4 == H + i, turn(own[base + i, :, NXD - 128 : NXD], 4 * i + 64 - 124), packed)
        pack_y[way] = packed
    strips = []
    edge = jnp.where(gy == tiles_y - 1, PYD - 1, 0)
    after = jnp.where(gy == tiles_y - 1, PYD - 2, 1)
    for first, wide, tile, beyond in ((0, 0, 0, 8), (126, 120, NXD - 128, 112)):
        packed = jnp.zeros((C, 128), F32)
        for m in range(PYD):
            packed = jnp.where(lane // 2 == 2 * PYD + m, turn(pown[m], 64 + 2 * m - first), packed)
        packed = jnp.where(lane // 8 == 6, turn(pown[edge], 48 - wide), packed)
        packed = jnp.where(lane // 8 == 7, turn(pown[after], 56 - wide), packed)
        for q, row in enumerate(RIM):
            packed = jnp.where(lane // 8 == 12 + q, turn(own[row, :, tile : tile + 128], 96 + 8 * q - beyond), packed)
        strips.append(packed)
    shores = []
    for base in (0, PYD - PH):
        packed = jnp.zeros((C, 128), F32)
        for i in range(PH):
            cells = pown[base + i]
            packed = jnp.where(lane // 2 == 24 + i, jnp.where(
                gx == 0, turn(cells, 48 + 2 * i), turn(cells, 48 + 2 * i - 126)), packed)
        shores.append(packed)

    wide_lane = lanes_of((C, NXD))
    inners = [(wide_lane >= n) & (wide_lane < NXD - n) for n in (4, NARROW)]
    spread = plane_tile(lambda c: diffusion[c])
    east_by = plane_tile(lambda c: drift[0, c])
    north_by = plane_tile(lambda c: drift[1, c])
    stay, cw, ce, cs, cn = factors(
        spread, east_by, north_by)
    middle = stay * stay + 2.0 * (cw * ce + cs * cn)

    def three(value):
        return jnp.concatenate([value] * (NXD // 128), axis=1)

    row_weights = [three(v) for v in (cw, stay, ce)]
    square_weights = [three(v) for v in (cw * cw, 2.0 * cw * stay, middle, 2.0 * stay * ce, ce * ce)]
    wind = jnp.zeros((C, PXD), F32)
    scale = jnp.zeros((C, PXD), F32)
    spot = jnp.zeros((C, PXD), F32)
    rests = [jnp.zeros((C, PXD), F32)] * 3

    def total(value):
        return jnp.sum(value, axis=1, keepdims=True)

    for s in range(MAXD):
        row, col = sites[0, 0, 0, s], sites[1, 0, 0, s]
        gap = wide_lane - col
        at_0 = gap == 0
        value = total(jnp.where(at_0, own[row], 0.0))
        wind = jnp.where(lane == s, value, wind)
        push = -(coef[0, 0, s] * live[0, 0, s].astype(F32))
        scale = jnp.where(lane == s, push, scale)
        spot = jnp.where(lane == MAXD + s, row.astype(F32), spot)
        spot = jnp.where(lane == 2 * MAXD + s, col.astype(F32), spot)
        spot = jnp.where(lane == 3 * MAXD + s, push, spot)
        line = jnp.where(gap == -1, row_weights[0], jnp.where(at_0, row_weights[1], jnp.where(gap == 1, row_weights[2], 0.0)))
        square = jnp.zeros((C, NXD), F32)
        for j in range(5):
            square = jnp.where(gap == j - 2, square_weights[j], square)
        at_rim = (gy == 0) & (row == 0) | (gy == tiles_y - 1) & (row == NYD - 1)
        second = jnp.where(at_rim, 0.0, 1.0)
        for inner, ways in ((inners[0], ((0, NEAR, NYD - 1, 1.0), (1, 0, NYD - 1 - NEAR, 1.0))),
                            (inners[1], ((2, 2, NYD - 3, second),))):
            near = {r: jnp.where(inner, own[jnp.clip(row + r, 0, NYD - 1)], 0.0) for r in range(-2, 3)}
            along = {r: total(line * near[r]) for r in range(-1, 2)}
            point = {r: total(jnp.where(at_0, near[r], 0.0)) for r in (-2, -1, 1, 2)}
            ones = {0: along[0], -1: cs * point[-1], 1: cn * point[1]}
            twos = {0: total(square * near[0]), -1: 2.0 * cs * along[-1], 1: 2.0 * cn * along[1],
                    -2: cs * cs * point[-2], 2: cn * cn * point[2]}
            for way, low, high, kept in ways:
                for terms, at, by in ((ones, 4 * MAXD + s, 1.0), (twos, 5 * MAXD + s, kept)):
                    value = jnp.zeros((C, 128), F32)
                    for r, term in terms.items():
                        value = value + term * ((row + r >= low) & (row + r <= high)).astype(F32)
                    rests[way] = jnp.where(lane == at, value * by, rests[way])
    mine = thrusts(wind, scale) + spot
    notes[0] = mine
    for i, extra in enumerate((rests[0] + shores[0], rests[1] + shores[1], rests[2] + strips[0], rests[2] + strips[1])):
        own_notes[i] = mine + extra

    for dx, dy, buffers in (
        (0, -1, (south, psouth, side.at[0])), (0, 1, (north, pnorth, side.at[1])), (-1, 0, (west,)), (1, 0, (east,)),
        (-1, -1, (corner.at[0],)), (1, -1, (corner.at[1],)), (-1, 1, (corner.at[2],)), (1, 1, (corner.at[3],)),
    ):
        @pl.when(jnp.logical_not(exists(dx, dy)))
        def _():
            for buffer in buffers + (notes.at[AROUND.index((dx, dy))],):
                buffer[...] = jnp.zeros(buffer.shape, F32)

    sends = [(own_notes.at[0 if dy < 0 else 1] if dx == 0 else own_notes.at[2 if dx < 0 else 3],
              notes.at[AROUND.index((-dx, -dy))], (dx, dy)) for dx, dy in AROUND[:0:-1]]
    sends += [
        (pown.at[pl.ds(PYD - PNEAR, PNEAR)], psouth, (0, 1)),
        (pown.at[pl.ds(0, PNEAR)], pnorth, (0, -1)),
        (pack_e.at[pl.ds(2, 2)], corner.at[0], (1, 1)),
        (pack_w.at[pl.ds(2, 2)], corner.at[1], (-1, 1)),
        (pack_e.at[pl.ds(0, 2)], corner.at[2], (1, -1)),
        (pack_w.at[pl.ds(0, 2)], corner.at[3], (-1, -1)),
        (strip_e, west, (1, 0)),
        (strip_w, east, (-1, 0)),
        (own.at[pl.ds(NYD - NEAR, NEAR)], south, (0, 1)),
        (own.at[pl.ds(0, NEAR)], north, (0, -1)),
        (pack_y.at[1], side.at[0], (0, 1)),
        (pack_y.at[0], side.at[1], (0, -1)),
    ]
    pl.semaphore_wait(barrier, around)
    copies = []
    for i, (source, target, (dx, dy)) in enumerate(sends):
        copy = pltpu.make_async_remote_copy(
            src_ref=source, dst_ref=target, send_sem=send_sem.at[i], recv_sem=recv_sem.at[i],
            device_id=device(dx, dy), device_id_type=MESH,
        )
        copies.append((copy, exists(dx, dy), exists(-dx, -dy)))
        pl.when(exists(dx, dy))(copy.start)
    def own_row(i, carry):
        tiles = [own[i, :, 128 * t : 128 * t + 128] for t in range(3)]
        up = [turn(v, 1) for v in tiles]
        down = [turn(v, -1) for v in tiles]
        below, above = own[jnp.maximum(i - 1, 0)], own[jnp.minimum(i + 1, NYD - 1)]
        below_by = cs * (i > 0).astype(F32)
        above_by = cn * (i < NYD - 1).astype(F32)
        for t in range(3):
            from_w = jnp.where(lane == 0, up[t - 1] if t > 0 else 0.0, up[t])
            from_e = jnp.where(lane == 127, down[t + 1] if t < 2 else 0.0, down[t])
            at = slice(128 * t, 128 * t + 128)
            two[H + i, :, at] = (stay * tiles[t] + cw * from_w + ce * from_e
                                 + below_by * below[:, at] + above_by * above[:, at])
        two[H + i, :, NXD:WIDE] = jnp.where(lane == 0, cw * up[2], jnp.where(lane == 127, ce * down[0], 0.0))
        return carry

    lax.fori_loop(0, NYD, own_row, 0, unroll=4)

    def clear(i, carry):
        two[i] = jnp.zeros((C, WIDE), F32)
        two[H + NYD + i] = jnp.zeros((C, WIDE), F32)
        return carry

    lax.fori_loop(0, H, clear, 0)

    early = len(AROUND) + 1
    for copy, sent, received in copies[:early]:
        pl.when(received)(copy.wait_recv)
    has_w, has_e = (gx > 0).astype(F32), (gx < tiles_x - 1).astype(F32)
    has_s, has_n = (gy > 0).astype(F32), (gy < tiles_y - 1).astype(F32)
    of_x = {-1: has_w, 0: None, 1: has_e}
    of_y = {-1: has_s, 0: None, 1: has_n}

    push = jnp.zeros((C, 128), F32)
    scale = jnp.zeros((C, 128), F32)
    disk_rows = jnp.full((C, 128), 1.0e6, F32)
    disk_cols = jnp.full((C, 128), 1.0e6, F32)
    missing = [jnp.zeros((C, 128), F32)] * 2
    for j, (dx, dy) in enumerate(AROUND):
        note = notes[j]
        here = lane // MAXD == j
        first, force = turn(note, MAXD * j), turn(note, MAXD * j - 3 * MAXD)
        for there in (of_x[dx], of_y[dy]):
            if there is not None:
                first, force = first * there, force * there
        if (dx == 0) != (dy == 0):
            missing = [jnp.where(here, turn(note, MAXD * j - (4 + i) * MAXD), missing[i]) for i in range(2)]
        push = jnp.where(here, first, push)
        scale = jnp.where(here, force, scale)
        disk_rows = jnp.where(here, turn(note, MAXD * j - MAXD) + float(H + NYD * dy), disk_rows)
        disk_cols = jnp.where(here, turn(note, MAXD * j - 2 * MAXD) + float(NXD * dx), disk_cols)

    def profile(distance):
        return jnp.where(jnp.abs(distance) <= float(FOOT), jnp.exp(distance * distance * (-1.0 / 8.0)), 0.0)

    rows_2 = thrice(disk_rows[0:8])
    height = lax.broadcasted_iota(jnp.int32, (8, 128), 0).astype(F32)
    for block in range(ROWS // 8):
        for half in range(2):
            value = profile(height + float(8 * block) - rows_2[half])
            for j in range(8):
                row_g[8 * block + j, :, 128 * half : 128 * half + 128] = value[j : j + 1]
    cols_2 = thrice(disk_cols[0:8])
    depth_at = lax.broadcasted_iota(jnp.int32, (128, 128), 0)
    for half in range(2):
        across = jnp.transpose(jnp.broadcast_to(cols_2[half][0:1], (128, 128)))
        third = depth_at + 128 * half >= 2 * SLOT
        for tile in range(WIDE // 128):
            at = lanes_of((128, 128)) + 128 * tile
            at = jnp.where(at < 448, at, at - WIDE).astype(F32)
            value = profile(at - across)
            rest = value - value.astype(BF16).astype(F32)
            col_g[128 * half : 128 * half + 128, 128 * tile : 128 * tile + 128] = jnp.where(third, rest, value).astype(BF16)
    scale_out[...] = scale
    for i in range(2):
        missing_out[i] = missing[i]

    low_side = jnp.where(gx == 0, 0, -64)
    high_side = jnp.where(gx == tiles_x - 1, NXD, NXD + 64)
    fine = lax.broadcasted_iota(jnp.int32, (WIDE, 128), 0)
    fine = jnp.where(fine < 448, fine, fine - WIDE)
    gap = jnp.abs(fine - (3 * lanes_of((WIDE, 128)) + 1))
    weight = jnp.where(gap <= 1, 2.0, jnp.where(gap <= 4, 1.0, 0.0))
    weight_out[...] = jnp.where((fine >= low_side) & (fine < high_side), weight, 0.0).astype(BF16)

    for block, (source, strip_w_in, strip_e_in, base, first, count) in enumerate((
        (psouth, notes[5], notes[6], 0, PH, PH),
        (pown, notes[3], notes[4], PH, 0, PYD),
        (pnorth, notes[7], notes[8], PH + PYD, 0, PH),
    )):
        for i in range(count):
            m = first + i
            if block == 0 and i < PH - PNEAR or block == 2 and i >= PNEAR:
                shore = notes[1 + block // 2]
                middle = jnp.where((lane < 2) & (gx == 0), turn(shore, -48 - 2 * i),
                                   jnp.where((lane >= 126) & (gx == tiles_x - 1), turn(shore, 78 - 2 * i), 0.0))
            else:
                middle = source[i - (PH - PNEAR) if block == 0 else i]
            old[base + i, :, 0:128] = middle
            old[base + i, :, 128:256] = jnp.where(
                lane < 2, turn(strip_e_in, -64 - 2 * m), jnp.where(lane >= 126, turn(strip_w_in, 62 - 2 * m), 0.0))

    @pl.when((gy == 0) | (gy == tiles_y - 1))
    def _():
        for i, at in enumerate((jnp.where(gy == 0, PH, PH + PYD - 1), jnp.where(gy == 0, PH + 1, PH + PYD - 2))):
            old[at, :, 128:256] = jnp.where(lane < 8, turn(notes[4], -48 - 8 * i), jnp.where(
                lane >= 120, turn(notes[3], 72 - 8 * i), 0.0))

    kept = jnp.where(lane < 64, has_e, has_w)
    stay, cw, ce, cs, cn = factors(spread * (1.0 / 3.0), east_by, north_by)
    new[0] = jnp.zeros((C, PWIDE), F32)
    new[PROWS - 1] = jnp.zeros((C, PWIDE), F32)

    def parent_row(i, carry):
        inside = jnp.where(i < PH, has_s, jnp.where(i >= PH + PYD, has_n, 1.0))
        tiles = [old[i, :, 128 * t : 128 * t + 128] for t in range(2)]
        from_w, from_e = shifted(tiles)
        for t in range(2):
            value = (stay * tiles[t] + cw * from_w[t] + ce * from_e[t]
                     + cs * old[i - 1, :, 128 * t : 128 * t + 128] + cn * old[i + 1, :, 128 * t : 128 * t + 128])
            value = value * inside
            new[i, :, 128 * t : 128 * t + 128] = value * kept if t == 1 else value
        return carry

    lax.fori_loop(1, PROWS - 1, parent_row, 0)

    @pl.when((gx == 0) | (gx == tiles_x - 1))
    def _():
        for source, target in ((old, cols_old), (new, cols_new)):
            for y in range(ROWS):
                q, rest = (y - H) // 3 + PH, (y - H) % 3
                centre = source[q, :, 0:128]
                if rest == 1:
                    value = centre * (2.0 / 3.0)
                else:
                    value = centre * (4.0 / 9.0) + source[q - 1 if rest == 0 else q + 1, :, 0:128] * (2.0 / 9.0)
                target[y] = value

    @pl.when((gy == 0) | (gy == tiles_y - 1))
    def _():
        fine = lanes_of((PWIDE, WIDE))
        fine = jnp.where(fine < 448, fine, fine - WIDE)
        coarse = lax.broadcasted_iota(jnp.int32, (PWIDE, WIDE), 0)
        coarse = jnp.where(coarse < 192, coarse, coarse - PWIDE)
        hat = jnp.maximum(3 - jnp.abs(fine - (3 * coarse + 1)), 0).astype(F32).astype(BF16)
        at = jnp.where(gy == 0, PH, PH + PYD - 1)
        parts = pieces(old[at], 3) + pieces(new[at], 3)
        for i in range(2):
            total = jnp.zeros((C, WIDE), F32)
            for part in parts[3 * i : 3 * i + 3]:
                total = total + jnp.dot(part, hat, preferred_element_type=F32)
            lines[i] = total * (2.0 / 9.0)

    amounts_2 = thrice(push)

    def first_force(i, carry):
        base = 1 + CHUNK * i
        force = force_rows(amounts_2, row_g, col_g, base)
        for r in range(CHUNK):
            two[base + r] += force[C * r : C * r + C]
        return carry

    lax.fori_loop(0, (ROWS - 2) // CHUNK, first_force, 0)

    for i, (copy, sent, received) in enumerate(copies):
        pl.when(sent)(copy.wait_send)
        if i >= early:
            pl.when(received)(copy.wait_recv)


def advance_all(tiles_x, tiles_y, diffusion, drift, own, south, north, west, east, corner, side, note_in,
                begun, new, cols_old, cols_new, lines, row_g, col_g, scale_in, missing, weight_in,
                nest_out, parent_out,
                one, two, places, out_v, sum_v, place_sem, out_sem):
    gx, gy = lax.axis_index("gx"), lax.axis_index("gy")
    lane = lanes_of((C, 128))
    notes = [note_in.at[j] for j in range(9)]
    moves = [pltpu.make_async_copy(note.at[pl.ds(0, 8)], places.at[j], place_sem.at[j]) for j, note in enumerate(notes)]
    for move in moves:
        move.start()
    has_s, has_n = (gy > 0).astype(F32), (gy < tiles_y - 1).astype(F32)
    scale = scale_in[...]

    def copy_rows(source, base, count):
        def body(i, carry):
            one[base + i, :, 0:NXD] = source[i]
            return carry
        lax.fori_loop(0, count, body, 0)

    copy_rows(south, H - NEAR, NEAR)
    one[H, :, 0:NXD] = own[0]
    one[H + NYD - 1, :, 0:NXD] = own[NYD - 1]
    copy_rows(north, H + NYD, NEAR)
    for p in range(ROWS // 8):
        for j in range(8):
            y = 8 * p + j
            row = y - H
            if 0 <= row < NYD:
                i = row % 16
                tile = jnp.where(lane < 8, turn(east[row // 16], -8 * i),
                                 jnp.where(lane >= 120, turn(west[row // 16], 120 - 8 * i), 0.0))
                if row in RIM:
                    q = RIM.index(row)
                    tile = jnp.where(lane // 8 == 1, turn(note_in[4], -88 - 8 * q), tile)
                    tile = jnp.where(lane // 8 == 14, turn(note_in[3], 16 - 8 * q), tile)
            else:
                way, i = (0, p) if y < H else (2, p - 8)
                tile = jnp.where(lane < 16, turn(corner[way + 1, i], -16 * j),
                                 jnp.where(lane >= 112, turn(corner[way, i], 112 - 16 * j), 0.0))
            one[y, :, NXD:WIDE] = tile
            if y < H - NEAR or y >= H + NYD + NEAR:
                way, i = (0, y) if y < H else (1, y - H - NYD)
                one[y, :, 0:128] = jnp.where(lane < 4, turn(side[way], -4 * i), 0.0)
                one[y, :, 128 : NXD - 128] = jnp.zeros((C, NXD - 256), F32)
                one[y, :, NXD - 128 : NXD] = jnp.where(lane >= 124, turn(side[way], 60 - 4 * i), 0.0)

    spread = plane_tile(lambda c: diffusion[c])
    east_by = plane_tile(lambda c: drift[0, c])
    north_by = plane_tile(lambda c: drift[1, c])

    stay, cw, ce, cs, cn = factors(spread, east_by, north_by)
    def swept(source, y):
        tiles = [source[y, :, 128 * t : 128 * t + 128] for t in range(4)]
        from_w, from_e = shifted(tiles)
        out = []
        for t in range(4):
            at = slice(128 * t, 128 * t + 128)
            out.append(stay * tiles[t] + cw * from_w[t] + ce * from_e[t]
                       + cs * source[y - 1, :, at] + cn * source[y + 1, :, at])
        return out

    def finish_first():
        def frame(i, carry):
            for y in (1 + i, H + NYD + i):
                for t, value in enumerate(swept(one, y)):
                    at = slice(128 * t, 128 * t + 128)
                    two[y, :, at] = begun[y, :, at] + value
            return carry

        lax.fori_loop(0, H - 1, frame, 0, unroll=3)

        def inside(i, carry):
            y = H + i
            tile = one[y, :, NXD:WIDE]
            up, down = turn(tile, 1), turn(tile, -1)
            two[y, :, 0:128] = begun[y, :, 0:128] + jnp.where(lane == 0, cw * up, 0.0)
            two[y, :, 128:256] = begun[y, :, 128:256]
            two[y, :, 256:384] = begun[y, :, 256:384] + jnp.where(lane == 127, ce * down, 0.0)
            two[y, :, NXD:WIDE] = (
                begun[y, :, NXD:WIDE] + stay * tile + jnp.where(lane == 0, 0.0, cw * up)
                + jnp.where(lane == 127, 0.0, ce * down) + cs * one[y - 1, :, NXD:WIDE] + cn * one[y + 1, :, NXD:WIDE])
            return carry

        lax.fori_loop(0, NYD, inside, 0, unroll=6)
        for y, by, beyond in ((H, cs, H - 1), (H + NYD - 1, cn, H + NYD)):
            for t in range(3):
                at = slice(128 * t, 128 * t + 128)
                two[y, :, at] += by * one[beyond, :, at]
        hold_edges(two, 1, ROWS - 1, 1)

    def hold_edges(target, low, high, k):
        for edge, tile, spot in ((0, 0, 0), (tiles_x - 1, NXD // 128 - 1, 127)):
            @pl.when(gx == edge)
            def _():
                def patch(i, carry):
                    at = slice(128 * tile, 128 * tile + 128)
                    bound = cols_old[i] + (k / 3.0) * (cols_new[i] - cols_old[i])
                    target[i, :, at] = jnp.where(lane == spot, bound, target[i, :, at])
                    return carry
                lax.fori_loop(low, high, patch, 0, unroll=6)
        for edge, row in ((0, H), (tiles_y - 1, H + NYD - 1)):
            @pl.when(gy == edge)
            def _():
                target[row] = lines[0] + (k / 3.0) * (lines[1] - lines[0])

    def step(source, target, amounts, low, high, k):
        amounts_2 = thrice(amounts)

        def body(i, carry):
            base = low + CHUNK * i
            force = force_rows(amounts_2, row_g, col_g, base)
            for r in range(CHUNK):
                for t, value in enumerate(swept(source, base + r)):
                    at = slice(128 * t, 128 * t + 128)
                    target[base + r, :, at] = value + force[C * r : C * r + C, at]
            return carry

        lax.fori_loop(0, (high - low) // CHUNK, body, 0, unroll=True)
        hold_edges(target, low, high, k)

    def gathered(source):
        wind = jnp.zeros((C, 128), F32)
        for j, (dx, dy) in enumerate(AROUND):
            for s in range(MAXD):
                d = MAXD * j + s
                row = places[j, 0, MAXD + s].astype(jnp.int32) + (H + NYD * dy)
                col = places[j, 0, 2 * MAXD + s].astype(jnp.int32) + NXD * dx
                row = jnp.clip(row, 0, ROWS - 1)
                col = jnp.bitwise_and(col, WIDE - 1)
                tile = pl.multiple_of(jnp.bitwise_and(col, WIDE - 128), 128)
                cells = source[row, :, pl.ds(tile, 128)]
                wind = jnp.where(lane == d, turn(cells, jnp.bitwise_and(d - col, 127)), wind)
        return wind

    for buffer, rows in ((two, (0, ROWS - 1)),):
        for row in rows:
            buffer[row] = jnp.zeros((C, WIDE), F32)

    finish_first()
    for move in moves:
        move.wait()
    push = thrusts(gathered(two) + missing[0], scale)
    step(two, one, push, 7, ROWS - 7, 2)
    push = thrusts(gathered(one) + missing[1], scale)
    step(one, two, push, 13, ROWS - 13, 3)

    stores = [pltpu.make_async_copy(two.at[pl.ds(H, NYD), c, pl.ds(0, NXD)], nest_out.at[c], out_sem.at[c]) for c in range(C)]
    for store in stores:
        store.start()

    def three(m):
        y = H + 3 * m
        return two[y] + two[y + 1] + two[y + 2]

    before, here = three(-1) * has_s, three(0)
    high_part, low_part = [], []
    for m in range(PYD):
        after = three(m + 1)
        if m == PYD - 1:
            after = after * has_n
        total = before + 2.0 * here + after
        part = pieces(total, 2)
        sum_v[C * m : C * m + C] = part[0]
        sum_v[C * (PYD + m) : C * (PYD + m) + C] = part[1]
        before, here = here, after
    mean = jnp.dot(sum_v[...], weight_in[...], preferred_element_type=F32)
    half = C * PYD
    for m in range(PYD):
        i = m + PH
        tiles = [new[i - 1, :, 128 * t : 128 * t + 128] + 2.0 * new[i, :, 128 * t : 128 * t + 128]
                 + new[i + 1, :, 128 * t : 128 * t + 128] for t in range(2)]
        from_w, from_e = shifted(tiles)
        direct = from_w[0] + 2.0 * tiles[0] + from_e[0]
        out_v[m] = direct * (1.0 / 32.0) + (mean[C * m : C * m + C] + mean[half + C * m : half + C * m + C]) * (1.0 / 288.0)
    last = [pltpu.make_async_copy(out_v.at[:, c, :], parent_out.at[c], out_sem.at[C + c]) for c in range(C)]
    for store in last:
        store.start()
    for store in stores + last:
        store.wait()


def solution(mesh):
    tiles_x, tiles_y = mesh.shape["gx"], mesh.shape["gy"]
    smem = pl.BlockSpec(memory_space=pltpu.SMEM)
    vmem = pl.BlockSpec(memory_space=pltpu.VMEM)
    anywhere = pl.BlockSpec(memory_space=pl.ANY)
    passed = ((NYD, C, NXD), (NEAR, C, NXD), (NEAR, C, NXD),
              (NYD // 16, C, 128), (NYD // 16, C, 128), (4, 2, C, 128), (2, C, 128), (9, C, 128),
              (ROWS, C, WIDE), (PROWS, C, PWIDE), (ROWS, C, 128), (ROWS, C, 128), (2, C, WIDE), (ROWS, 1, 256),
              (256, WIDE), (C, 128), (2, C, 128), (WIDE, 128))
    halved = (14, 17)

    def on_device(nest_wind, parent_wind, diffusion, drift, disk_sites, disk_live, disk_coef):
        rims = pl.pallas_call(
            functools.partial(exchange, tiles_x, tiles_y),
            out_shape=[pltpu.VMEM(shape, BF16 if i in halved else F32) for i, shape in enumerate(passed)],
            in_specs=[pl.BlockSpec(memory_space=pltpu.HBM)] * 7,
            out_specs=[vmem] * len(passed),
            scratch_shapes=[
                pltpu.VMEM((PYD, C, PXD), F32),
                pltpu.VMEM((PNEAR, C, PXD), F32),
                pltpu.VMEM((PNEAR, C, PXD), F32),
                pltpu.VMEM((PROWS, C, PWIDE), F32),
                pltpu.VMEM((NYD // 16, C, 128), F32),
                pltpu.VMEM((NYD // 16, C, 128), F32),
                pltpu.VMEM((4, C, 128), F32),
                pltpu.VMEM((4, C, 128), F32),
                pltpu.VMEM((2, C, 128), F32),
                pltpu.VMEM((4, C, 128), F32),
                pltpu.SMEM(diffusion.shape, F32),
                pltpu.SMEM(drift.shape, F32),
                pltpu.SMEM((2, 1, 1, MAXD), jnp.int32),
                pltpu.SMEM((1, 1, MAXD), jnp.int32),
                pltpu.SMEM((1, 1, MAXD), F32),
                pltpu.SemaphoreType.DMA((2 * C + 5,)),
                pltpu.SemaphoreType.DMA((20,)),
                pltpu.SemaphoreType.DMA((20,)),
            ],
            compiler_params=pltpu.CompilerParams(
                collective_id=0, has_side_effects=True, vmem_limit_bytes=16 * 2**20),
            name="exchange",
        )(*[pltpu.with_memory_space_constraint(x, pltpu.HBM) for x in
            (nest_wind, parent_wind, diffusion, drift, disk_sites, disk_live, disk_coef)])
        return tuple(pl.pallas_call(
            functools.partial(advance_all, tiles_x, tiles_y),
            out_shape=[jax.ShapeDtypeStruct(nest_wind.shape, F32), jax.ShapeDtypeStruct(parent_wind.shape, F32)],
            in_specs=[smem, smem] + [vmem] * len(passed),
            out_specs=[anywhere, anywhere],
            scratch_shapes=[
                pltpu.VMEM((ROWS, C, WIDE), F32),
                pltpu.VMEM((ROWS, C, WIDE), F32),
                pltpu.SMEM((9, 8, 128), F32),
                pltpu.VMEM((PYD, C, PXD), F32),
                pltpu.VMEM((2 * C * PYD, WIDE), BF16),
                pltpu.SemaphoreType.DMA((9,)),
                pltpu.SemaphoreType.DMA((2 * C,)),
            ],
            compiler_params=pltpu.CompilerParams(vmem_limit_bytes=40 * 2**20),
            name="advance",
        )(diffusion, drift, *rims))

    placed = (
        P(None, "gy", "gx"),
        P(None, "gy", "gx"),
        P(),
        P(),
        P(None, "gy", "gx", None),
        P("gy", "gx", None),
        P("gy", "gx", None),
    )
    return jax.shard_map(
        on_device,
        mesh=mesh,
        in_specs=placed,
        out_specs=(P(None, "gy", "gx"), P(None, "gy", "gx")),
        check_vma=False,
    )
```

```python
import functools

import jax
import jax.numpy as jnp
from jax import lax
from jax.experimental import pallas as pl
from jax.experimental.pallas import tpu as pltpu
from jax.sharding import PartitionSpec as P

C = 16
NYD = 48
NXD = 384
PYD = 16
PXD = 128
MAXD = 8
FOOT = 6
H = 16
PH = 8
NEAR = 6
PNEAR = 2
NARROW = 8
RIM = (0, 1, NYD - 2, NYD - 1)
ROWS = NYD + 2 * H
PROWS = PYD + 2 * PH
WIDE = 512
PWIDE = 256
SLOT = 80
CHUNK = 6
F32 = jnp.float32
BF16 = jnp.bfloat16
MESH = pl.DeviceIdType.MESH
AROUND = ((0, 0), (0, -1), (0, 1), (-1, 0), (1, 0), (-1, -1), (1, -1), (-1, 1), (1, 1))


def lanes_of(shape):
    return lax.broadcasted_iota(jnp.int32, shape, len(shape) - 1)


def turn(value, shift):
    shift = shift % value.shape[-1] if isinstance(shift, int) else shift
    if isinstance(shift, int) and shift == 0:
        return value
    return pltpu.roll(value, shift, value.ndim - 1)


def thrusts(wind, scale):
    half = C // 2
    east, north = wind[:half], wind[half:]
    speed = jnp.sqrt(east * east + north * north + 1.0)
    return scale * wind * jnp.concatenate([speed, speed], axis=0)


def plane_tile(read):
    at = lax.broadcasted_iota(jnp.int32, (C, 128), 0)
    value = jnp.zeros((C, 128), F32)
    for c in range(C):
        value = jnp.where(at == c, read(c), value)
    return value


def factors(spread, east_by, north_by):
    return (1.0 - 4.0 * spread - east_by - north_by, spread + east_by, spread, spread + north_by, spread)


def shifted(tiles):
    lane = lanes_of((C, 128))
    count = len(tiles)
    up = [turn(v, 1) for v in tiles]
    down = [turn(v, -1) for v in tiles]
    from_w = [jnp.where(lane == 0, up[(t - 1) % count], up[t]) for t in range(count)]
    from_e = [jnp.where(lane == 127, down[(t + 1) % count], down[t]) for t in range(count)]
    return from_w, from_e


def pieces(value, count):
    out = []
    for _ in range(count):
        part = value.astype(BF16)
        out.append(part)
        value = value - part.astype(F32)
    return out


def thrice(value):
    shape = value.shape
    at = lanes_of(shape)
    later = turn(value, SLOT)
    return (jnp.where(at < SLOT, value, later),
            jnp.where(at < 2 * SLOT - 128, later, turn(value, 2 * SLOT - 128)))


def force_rows(amounts_2, row_g, col_g, base):
    at = lanes_of((C, 128))
    second = (at >= SLOT, at < 2 * SLOT - 128)
    left = []
    for r in range(CHUNK):
        halves = []
        for half in range(2):
            value = amounts_2[half] * row_g[base + r, :, 128 * half : 128 * half + 128]
            rest = value - value.astype(BF16).astype(F32)
            halves.append(jnp.where(second[half], rest, value).astype(BF16))
        left.append(jnp.concatenate(halves, axis=1))
    return jnp.dot(jnp.concatenate(left, axis=0), col_g[...], preferred_element_type=F32)


def exchange(tiles_x, tiles_y, nest, parent, diffusion_h, drift_h, sites_h, live_h, coef_h,
             own, south, north, west, east, corner, side, notes,
             two, new, cols_old, cols_new, lines, row_g, col_g, scale_out, missing_out, weight_out,
             pown, psouth, pnorth, old, strip_w, strip_e, pack_w, pack_e, pack_y, own_notes, diffusion, drift, sites, live, coef, in_sem, send_sem, recv_sem):
    gx, gy = lax.axis_index("gx"), lax.axis_index("gy")

    def device(dx, dy):
        return (lax.rem(gx + dx + tiles_x, tiles_x), lax.rem(gy + dy + tiles_y, tiles_y))

    def exists(dx, dy):
        at_x, at_y = gx + dx, gy + dy
        return (at_x >= 0) & (at_x < tiles_x) & (at_y >= 0) & (at_y < tiles_y)

    barrier = pltpu.get_barrier_semaphore()
    around = 0
    for dx, dy in AROUND[1:]:
        around = around + exists(dx, dy).astype(jnp.int32)

        @pl.when(exists(dx, dy))
        def _():
            pl.semaphore_signal(barrier, inc=1, device_id=device(dx, dy), device_id_type=MESH)

    small = ((diffusion_h, diffusion), (drift_h, drift), (sites_h, sites), (live_h, live), (coef_h, coef))
    loads = [pltpu.make_async_copy(nest.at[c], own.at[:, c, :], in_sem.at[c]) for c in range(C)]
    loads += [pltpu.make_async_copy(parent.at[c], pown.at[:, c, :], in_sem.at[C + c]) for c in range(C)]
    loads += [pltpu.make_async_copy(a, b, in_sem.at[2 * C + i]) for i, (a, b) in enumerate(small)]
    for load in loads:
        load.start()
    for load in loads:
        load.wait()

    lane = lanes_of((C, PXD))
    for pack, tile, first in ((pack_w, 0, 0), (pack_e, NXD // 128 - 1, 112)):
        for i, p in enumerate((0, 1, 4, 5)):
            packed = jnp.zeros((C, 128), F32)
            for j in range(8):
                cells = own[8 * p + j, :, 128 * tile : 128 * tile + 128]
                packed = jnp.where(lane // 16 == j, turn(cells, 16 * j - first), packed)
            pack[i] = packed
    for strip, tile, first in ((strip_w, 0, 0), (strip_e, NXD // 128 - 1, 120)):
        for p in range(NYD // 16):
            packed = jnp.zeros((C, 128), F32)
            for j in range(16):
                cells = own[16 * p + j, :, 128 * tile : 128 * tile + 128]
                packed = jnp.where(lane // 8 == j, turn(cells, 8 * j - first), packed)
            strip[p] = packed
    for way, base in ((0, 0), (1, NYD - H)):
        packed = jnp.zeros((C, 128), F32)
        for i in range(H):
            packed = jnp.where(lane // 4 == i, turn(own[base + i, :, 0:128], 4 * i), packed)
            packed = jnp.where(lane // 4 == H + i, turn(own[base + i, :, NXD - 128 : NXD], 4 * i + 64 - 124), packed)
        pack_y[way] = packed
    strips = []
    edge = jnp.where(gy == tiles_y - 1, PYD - 1, 0)
    after = jnp.where(gy == tiles_y - 1, PYD - 2, 1)
    for first, wide, tile, beyond in ((0, 0, 0, 8), (126, 120, NXD - 128, 112)):
        packed = jnp.zeros((C, 128), F32)
        for m in range(PYD):
            packed = jnp.where(lane // 2 == 2 * PYD + m, turn(pown[m], 64 + 2 * m - first), packed)
        packed = jnp.where(lane // 8 == 6, turn(pown[edge], 48 - wide), packed)
        packed = jnp.where(lane // 8 == 7, turn(pown[after], 56 - wide), packed)
        for q, row in enumerate(RIM):
            packed = jnp.where(lane // 8 == 12 + q, turn(own[row, :, tile : tile + 128], 96 + 8 * q - beyond), packed)
        strips.append(packed)
    shores = []
    for base in (0, PYD - PH):
        packed = jnp.zeros((C, 128), F32)
        for i in range(PH):
            cells = pown[base + i]
            packed = jnp.where(lane // 2 == 24 + i, jnp.where(
                gx == 0, turn(cells, 48 + 2 * i), turn(cells, 48 + 2 * i - 126)), packed)
        shores.append(packed)

    wide_lane = lanes_of((C, NXD))
    inners = [(wide_lane >= n) & (wide_lane < NXD - n) for n in (4, NARROW)]
    spread = plane_tile(lambda c: diffusion[c])
    east_by = plane_tile(lambda c: drift[0, c])
    north_by = plane_tile(lambda c: drift[1, c])
    stay, cw, ce, cs, cn = factors(
        spread, east_by, north_by)
    middle = stay * stay + 2.0 * (cw * ce + cs * cn)

    def three(value):
        return jnp.concatenate([value] * (NXD // 128), axis=1)

    row_weights = [three(v) for v in (cw, stay, ce)]
    square_weights = [three(v) for v in (cw * cw, 2.0 * cw * stay, middle, 2.0 * stay * ce, ce * ce)]
    wind = jnp.zeros((C, PXD), F32)
    scale = jnp.zeros((C, PXD), F32)
    spot = jnp.zeros((C, PXD), F32)
    rests = [jnp.zeros((C, PXD), F32)] * 3

    def total(value):
        return jnp.sum(value, axis=1, keepdims=True)

    for s in range(MAXD):
        row, col = sites[0, 0, 0, s], sites[1, 0, 0, s]
        gap = wide_lane - col
        at_0 = gap == 0
        value = total(jnp.where(at_0, own[row], 0.0))
        wind = jnp.where(lane == s, value, wind)
        push = -(coef[0, 0, s] * live[0, 0, s].astype(F32))
        scale = jnp.where(lane == s, push, scale)
        spot = jnp.where(lane == MAXD + s, row.astype(F32), spot)
        spot = jnp.where(lane == 2 * MAXD + s, col.astype(F32), spot)
        spot = jnp.where(lane == 3 * MAXD + s, push, spot)
        line = jnp.where(gap == -1, row_weights[0], jnp.where(at_0, row_weights[1], jnp.where(gap == 1, row_weights[2], 0.0)))
        square = jnp.zeros((C, NXD), F32)
        for j in range(5):
            square = jnp.where(gap == j - 2, square_weights[j], square)
        at_rim = (gy == 0) & (row == 0) | (gy == tiles_y - 1) & (row == NYD - 1)
        second = jnp.where(at_rim, 0.0, 1.0)
        for inner, ways in ((inners[0], ((0, NEAR, NYD - 1, 1.0), (1, 0, NYD - 1 - NEAR, 1.0))),
                            (inners[1], ((2, 2, NYD - 3, second),))):
            near = {r: jnp.where(inner, own[jnp.clip(row + r, 0, NYD - 1)], 0.0) for r in range(-2, 3)}
            along = {r: total(line * near[r]) for r in range(-1, 2)}
            point = {r: total(jnp.where(at_0, near[r], 0.0)) for r in (-2, -1, 1, 2)}
            ones = {0: along[0], -1: cs * point[-1], 1: cn * point[1]}
            twos = {0: total(square * near[0]), -1: 2.0 * cs * along[-1], 1: 2.0 * cn * along[1],
                    -2: cs * cs * point[-2], 2: cn * cn * point[2]}
            for way, low, high, kept in ways:
                for terms, at, by in ((ones, 4 * MAXD + s, 1.0), (twos, 5 * MAXD + s, kept)):
                    value = jnp.zeros((C, 128), F32)
                    for r, term in terms.items():
                        value = value + term * ((row + r >= low) & (row + r <= high)).astype(F32)
                    rests[way] = jnp.where(lane == at, value * by, rests[way])
    mine = thrusts(wind, scale) + spot
    notes[0] = mine
    for i, extra in enumerate((rests[0] + shores[0], rests[1] + shores[1], rests[2] + strips[0], rests[2] + strips[1])):
        own_notes[i] = mine + extra

    for dx, dy, buffers in (
        (0, -1, (south, psouth, side.at[0])), (0, 1, (north, pnorth, side.at[1])), (-1, 0, (west,)), (1, 0, (east,)),
        (-1, -1, (corner.at[0],)), (1, -1, (corner.at[1],)), (-1, 1, (corner.at[2],)), (1, 1, (corner.at[3],)),
    ):
        @pl.when(jnp.logical_not(exists(dx, dy)))
        def _():
            for buffer in buffers + (notes.at[AROUND.index((dx, dy))],):
                buffer[...] = jnp.zeros(buffer.shape, F32)

    sends = [(own_notes.at[0 if dy < 0 else 1] if dx == 0 else own_notes.at[2 if dx < 0 else 3],
              notes.at[AROUND.index((-dx, -dy))], (dx, dy)) for dx, dy in AROUND[:0:-1]]
    sends += [
        (pown.at[pl.ds(PYD - PNEAR, PNEAR)], psouth, (0, 1)),
        (pown.at[pl.ds(0, PNEAR)], pnorth, (0, -1)),
        (pack_e.at[pl.ds(2, 2)], corner.at[0], (1, 1)),
        (pack_w.at[pl.ds(2, 2)], corner.at[1], (-1, 1)),
        (pack_e.at[pl.ds(0, 2)], corner.at[2], (1, -1)),
        (pack_w.at[pl.ds(0, 2)], corner.at[3], (-1, -1)),
        (strip_e, west, (1, 0)),
        (strip_w, east, (-1, 0)),
        (own.at[pl.ds(NYD - NEAR, NEAR)], south, (0, 1)),
        (own.at[pl.ds(0, NEAR)], north, (0, -1)),
        (pack_y.at[1], side.at[0], (0, 1)),
        (pack_y.at[0], side.at[1], (0, -1)),
    ]
    pl.semaphore_wait(barrier, around)
    copies = []
    for i, (source, target, (dx, dy)) in enumerate(sends):
        copy = pltpu.make_async_remote_copy(
            src_ref=source, dst_ref=target, send_sem=send_sem.at[i], recv_sem=recv_sem.at[i],
            device_id=device(dx, dy), device_id_type=MESH,
        )
        copies.append((copy, exists(dx, dy), exists(-dx, -dy)))
        pl.when(exists(dx, dy))(copy.start)
    def own_row(i, carry):
        tiles = [own[i, :, 128 * t : 128 * t + 128] for t in range(3)]
        up = [turn(v, 1) for v in tiles]
        down = [turn(v, -1) for v in tiles]
        below, above = own[jnp.maximum(i - 1, 0)], own[jnp.minimum(i + 1, NYD - 1)]
        below_by = cs * (i > 0).astype(F32)
        above_by = cn * (i < NYD - 1).astype(F32)
        for t in range(3):
            from_w = jnp.where(lane == 0, up[t - 1] if t > 0 else 0.0, up[t])
            from_e = jnp.where(lane == 127, down[t + 1] if t < 2 else 0.0, down[t])
            at = slice(128 * t, 128 * t + 128)
            two[H + i, :, at] = (stay * tiles[t] + cw * from_w + ce * from_e
                                 + below_by * below[:, at] + above_by * above[:, at])
        two[H + i, :, NXD:WIDE] = jnp.where(lane == 0, cw * up[2], jnp.where(lane == 127, ce * down[0], 0.0))
        return carry

    lax.fori_loop(0, NYD, own_row, 0, unroll=4)

    def clear(i, carry):
        two[i] = jnp.zeros((C, WIDE), F32)
        two[H + NYD + i] = jnp.zeros((C, WIDE), F32)
        return carry

    lax.fori_loop(0, H, clear, 0)

    early = len(AROUND) + 1
    for copy, sent, received in copies[:early]:
        pl.when(received)(copy.wait_recv)
    has_w, has_e = (gx > 0).astype(F32), (gx < tiles_x - 1).astype(F32)
    has_s, has_n = (gy > 0).astype(F32), (gy < tiles_y - 1).astype(F32)
    of_x = {-1: has_w, 0: None, 1: has_e}
    of_y = {-1: has_s, 0: None, 1: has_n}

    push = jnp.zeros((C, 128), F32)
    scale = jnp.zeros((C, 128), F32)
    disk_rows = jnp.full((C, 128), 1.0e6, F32)
    disk_cols = jnp.full((C, 128), 1.0e6, F32)
    missing = [jnp.zeros((C, 128), F32)] * 2
    for j, (dx, dy) in enumerate(AROUND):
        note = notes[j]
        here = lane // MAXD == j
        first, force = turn(note, MAXD * j), turn(note, MAXD * j - 3 * MAXD)
        for there in (of_x[dx], of_y[dy]):
            if there is not None:
                first, force = first * there, force * there
        if (dx == 0) != (dy == 0):
            missing = [jnp.where(here, turn(note, MAXD * j - (4 + i) * MAXD), missing[i]) for i in range(2)]
        push = jnp.where(here, first, push)
        scale = jnp.where(here, force, scale)
        disk_rows = jnp.where(here, turn(note, MAXD * j - MAXD) + float(H + NYD * dy), disk_rows)
        disk_cols = jnp.where(here, turn(note, MAXD * j - 2 * MAXD) + float(NXD * dx), disk_cols)

    def profile(distance):
        return jnp.where(jnp.abs(distance) <= float(FOOT), jnp.exp(distance * distance * (-1.0 / 8.0)), 0.0)

    rows_2 = thrice(disk_rows[0:8])
    height = lax.broadcasted_iota(jnp.int32, (8, 128), 0).astype(F32)
    for block in range(ROWS // 8):
        for half in range(2):
            value = profile(height + float(8 * block) - rows_2[half])
            for j in range(8):
                row_g[8 * block + j, :, 128 * half : 128 * half + 128] = value[j : j + 1]
    cols_2 = thrice(disk_cols[0:8])
    depth_at = lax.broadcasted_iota(jnp.int32, (128, 128), 0)
    for half in range(2):
        across = jnp.transpose(jnp.broadcast_to(cols_2[half][0:1], (128, 128)))
        third = depth_at + 128 * half >= 2 * SLOT
        for tile in range(WIDE // 128):
            at = lanes_of((128, 128)) + 128 * tile
            at = jnp.where(at < 448, at, at - WIDE).astype(F32)
            value = profile(at - across)
            rest = value - value.astype(BF16).astype(F32)
            col_g[128 * half : 128 * half + 128, 128 * tile : 128 * tile + 128] = jnp.where(third, rest, value).astype(BF16)
    scale_out[...] = scale
    for i in range(2):
        missing_out[i] = missing[i]

    low_side = jnp.where(gx == 0, 0, -64)
    high_side = jnp.where(gx == tiles_x - 1, NXD, NXD + 64)
    fine = lax.broadcasted_iota(jnp.int32, (WIDE, 128), 0)
    fine = jnp.where(fine < 448, fine, fine - WIDE)
    gap = jnp.abs(fine - (3 * lanes_of((WIDE, 128)) + 1))
    weight = jnp.where(gap <= 1, 2.0, jnp.where(gap <= 4, 1.0, 0.0))
    weight_out[...] = jnp.where((fine >= low_side) & (fine < high_side), weight, 0.0).astype(BF16)

    for block, (source, strip_w_in, strip_e_in, base, first, count) in enumerate((
        (psouth, notes[5], notes[6], 0, PH, PH),
        (pown, notes[3], notes[4], PH, 0, PYD),
        (pnorth, notes[7], notes[8], PH + PYD, 0, PH),
    )):
        for i in range(count):
            m = first + i
            if block == 0 and i < PH - PNEAR or block == 2 and i >= PNEAR:
                shore = notes[1 + block // 2]
                middle = jnp.where((lane < 2) & (gx == 0), turn(shore, -48 - 2 * i),
                                   jnp.where((lane >= 126) & (gx == tiles_x - 1), turn(shore, 78 - 2 * i), 0.0))
            else:
                middle = source[i - (PH - PNEAR) if block == 0 else i]
            old[base + i, :, 0:128] = middle
            old[base + i, :, 128:256] = jnp.where(
                lane < 2, turn(strip_e_in, -64 - 2 * m), jnp.where(lane >= 126, turn(strip_w_in, 62 - 2 * m), 0.0))

    @pl.when((gy == 0) | (gy == tiles_y - 1))
    def _():
        for i, at in enumerate((jnp.where(gy == 0, PH, PH + PYD - 1), jnp.where(gy == 0, PH + 1, PH + PYD - 2))):
            old[at, :, 128:256] = jnp.where(lane < 8, turn(notes[4], -48 - 8 * i), jnp.where(
                lane >= 120, turn(notes[3], 72 - 8 * i), 0.0))

    kept = jnp.where(lane < 64, has_e, has_w)
    stay, cw, ce, cs, cn = factors(spread * (1.0 / 3.0), east_by, north_by)
    new[0] = jnp.zeros((C, PWIDE), F32)
    new[PROWS - 1] = jnp.zeros((C, PWIDE), F32)

    def parent_row(i, carry):
        inside = jnp.where(i < PH, has_s, jnp.where(i >= PH + PYD, has_n, 1.0))
        tiles = [old[i, :, 128 * t : 128 * t + 128] for t in range(2)]
        from_w, from_e = shifted(tiles)
        for t in range(2):
            value = (stay * tiles[t] + cw * from_w[t] + ce * from_e[t]
                     + cs * old[i - 1, :, 128 * t : 128 * t + 128] + cn * old[i + 1, :, 128 * t : 128 * t + 128])
            value = value * inside
            new[i, :, 128 * t : 128 * t + 128] = value * kept if t == 1 else value
        return carry

    lax.fori_loop(1, PROWS - 1, parent_row, 0)

    @pl.when((gx == 0) | (gx == tiles_x - 1))
    def _():
        for source, target in ((old, cols_old), (new, cols_new)):
            for y in range(ROWS):
                q, rest = (y - H) // 3 + PH, (y - H) % 3
                centre = source[q, :, 0:128]
                if rest == 1:
                    value = centre * (2.0 / 3.0)
                else:
                    value = centre * (4.0 / 9.0) + source[q - 1 if rest == 0 else q + 1, :, 0:128] * (2.0 / 9.0)
                target[y] = value

    @pl.when((gy == 0) | (gy == tiles_y - 1))
    def _():
        fine = lanes_of((PWIDE, WIDE))
        fine = jnp.where(fine < 448, fine, fine - WIDE)
        coarse = lax.broadcasted_iota(jnp.int32, (PWIDE, WIDE), 0)
        coarse = jnp.where(coarse < 192, coarse, coarse - PWIDE)
        hat = jnp.maximum(3 - jnp.abs(fine - (3 * coarse + 1)), 0).astype(F32).astype(BF16)
        at = jnp.where(gy == 0, PH, PH + PYD - 1)
        parts = pieces(old[at], 3) + pieces(new[at], 3)
        for i in range(2):
            total = jnp.zeros((C, WIDE), F32)
            for part in parts[3 * i : 3 * i + 3]:
                total = total + jnp.dot(part, hat, preferred_element_type=F32)
            lines[i] = total * (2.0 / 9.0)

    amounts_2 = thrice(push)

    def first_force(i, carry):
        base = 1 + CHUNK * i
        force = force_rows(amounts_2, row_g, col_g, base)
        for r in range(CHUNK):
            two[base + r] += force[C * r : C * r + C]
        return carry

    lax.fori_loop(0, (ROWS - 2) // CHUNK, first_force, 0)

    for i, (copy, sent, received) in enumerate(copies):
        pl.when(sent)(copy.wait_send)
        if i >= early:
            pl.when(received)(copy.wait_recv)


def advance_all(tiles_x, tiles_y, diffusion, drift, own, south, north, west, east, corner, side, note_in,
                begun, new, cols_old, cols_new, lines, row_g, col_g, scale_in, missing, weight_in,
                nest_out, parent_out,
                one, two, places, out_v, sum_v, place_sem, out_sem):
    gx, gy = lax.axis_index("gx"), lax.axis_index("gy")
    lane = lanes_of((C, 128))
    notes = [note_in.at[j] for j in range(9)]
    moves = [pltpu.make_async_copy(note.at[pl.ds(0, 8)], places.at[j], place_sem.at[j]) for j, note in enumerate(notes)]
    for move in moves:
        move.start()
    has_s, has_n = (gy > 0).astype(F32), (gy < tiles_y - 1).astype(F32)
    scale = scale_in[...]

    def copy_rows(source, base, count):
        def body(i, carry):
            one[base + i, :, 0:NXD] = source[i]
            return carry
        lax.fori_loop(0, count, body, 0)

    copy_rows(south, H - NEAR, NEAR)
    one[H, :, 0:NXD] = own[0]
    one[H + NYD - 1, :, 0:NXD] = own[NYD - 1]
    copy_rows(north, H + NYD, NEAR)
    for p in range(ROWS // 8):
        for j in range(8):
            y = 8 * p + j
            row = y - H
            if 0 <= row < NYD:
                i = row % 16
                tile = jnp.where(lane < 8, turn(east[row // 16], -8 * i),
                                 jnp.where(lane >= 120, turn(west[row // 16], 120 - 8 * i), 0.0))
                if row in RIM:
                    q = RIM.index(row)
                    tile = jnp.where(lane // 8 == 1, turn(note_in[4], -88 - 8 * q), tile)
                    tile = jnp.where(lane // 8 == 14, turn(note_in[3], 16 - 8 * q), tile)
            else:
                way, i = (0, p) if y < H else (2, p - 8)
                tile = jnp.where(lane < 16, turn(corner[way + 1, i], -16 * j),
                                 jnp.where(lane >= 112, turn(corner[way, i], 112 - 16 * j), 0.0))
            one[y, :, NXD:WIDE] = tile
            if y < H - NEAR or y >= H + NYD + NEAR:
                way, i = (0, y) if y < H else (1, y - H - NYD)
                one[y, :, 0:128] = jnp.where(lane < 4, turn(side[way], -4 * i), 0.0)
                one[y, :, 128 : NXD - 128] = jnp.zeros((C, NXD - 256), F32)
                one[y, :, NXD - 128 : NXD] = jnp.where(lane >= 124, turn(side[way], 60 - 4 * i), 0.0)

    spread = plane_tile(lambda c: diffusion[c])
    east_by = plane_tile(lambda c: drift[0, c])
    north_by = plane_tile(lambda c: drift[1, c])

    stay, cw, ce, cs, cn = factors(spread, east_by, north_by)
    def swept(source, y):
        tiles = [source[y, :, 128 * t : 128 * t + 128] for t in range(4)]
        from_w, from_e = shifted(tiles)
        out = []
        for t in range(4):
            at = slice(128 * t, 128 * t + 128)
            out.append(stay * tiles[t] + cw * from_w[t] + ce * from_e[t]
                       + cs * source[y - 1, :, at] + cn * source[y + 1, :, at])
        return out

    def finish_first():
        def frame(i, carry):
            for y in (1 + i, H + NYD + i):
                for t, value in enumerate(swept(one, y)):
                    at = slice(128 * t, 128 * t + 128)
                    two[y, :, at] = begun[y, :, at] + value
            return carry

        lax.fori_loop(0, H - 1, frame, 0, unroll=True)

        def inside(i, carry):
            y = H + i
            tile = one[y, :, NXD:WIDE]
            up, down = turn(tile, 1), turn(tile, -1)
            two[y, :, 0:128] = begun[y, :, 0:128] + jnp.where(lane == 0, cw * up, 0.0)
            two[y, :, 128:256] = begun[y, :, 128:256]
            two[y, :, 256:384] = begun[y, :, 256:384] + jnp.where(lane == 127, ce * down, 0.0)
            two[y, :, NXD:WIDE] = (
                begun[y, :, NXD:WIDE] + stay * tile + jnp.where(lane == 0, 0.0, cw * up)
                + jnp.where(lane == 127, 0.0, ce * down) + cs * one[y - 1, :, NXD:WIDE] + cn * one[y + 1, :, NXD:WIDE])
            return carry

        lax.fori_loop(0, NYD, inside, 0, unroll=True)
        for y, by, beyond in ((H, cs, H - 1), (H + NYD - 1, cn, H + NYD)):
            for t in range(3):
                at = slice(128 * t, 128 * t + 128)
                two[y, :, at] += by * one[beyond, :, at]
        hold_edges(two, 1, ROWS - 1, 1)

    def hold_edges(target, low, high, k):
        for edge, tile, spot in ((0, 0, 0), (tiles_x - 1, NXD // 128 - 1, 127)):
            @pl.when(gx == edge)
            def _():
                def patch(i, carry):
                    at = slice(128 * tile, 128 * tile + 128)
                    bound = cols_old[i] + (k / 3.0) * (cols_new[i] - cols_old[i])
                    target[i, :, at] = jnp.where(lane == spot, bound, target[i, :, at])
                    return carry
                lax.fori_loop(low, high, patch, 0, unroll=6)
        for edge, row in ((0, H), (tiles_y - 1, H + NYD - 1)):
            @pl.when(gy == edge)
            def _():
                target[row] = lines[0] + (k / 3.0) * (lines[1] - lines[0])

    def step(source, target, amounts, low, high, k):
        amounts_2 = thrice(amounts)

        def body(i, carry):
            base = low + CHUNK * i
            force = force_rows(amounts_2, row_g, col_g, base)
            for r in range(CHUNK):
                for t, value in enumerate(swept(source, base + r)):
                    at = slice(128 * t, 128 * t + 128)
                    target[base + r, :, at] = value + force[C * r : C * r + C, at]
            return carry

        lax.fori_loop(0, (high - low) // CHUNK, body, 0, unroll=True)
        hold_edges(target, low, high, k)

    def gathered(source):
        wind = jnp.zeros((C, 128), F32)
        for j, (dx, dy) in enumerate(AROUND):
            for s in range(MAXD):
                d = MAXD * j + s
                row = places[j, 0, MAXD + s].astype(jnp.int32) + (H + NYD * dy)
                col = places[j, 0, 2 * MAXD + s].astype(jnp.int32) + NXD * dx
                row = jnp.clip(row, 0, ROWS - 1)
                col = jnp.bitwise_and(col, WIDE - 1)
                tile = pl.multiple_of(jnp.bitwise_and(col, WIDE - 128), 128)
                cells = source[row, :, pl.ds(tile, 128)]
                wind = jnp.where(lane == d, turn(cells, jnp.bitwise_and(d - col, 127)), wind)
        return wind

    for buffer, rows in ((two, (0, ROWS - 1)),):
        for row in rows:
            buffer[row] = jnp.zeros((C, WIDE), F32)

    finish_first()
    for move in moves:
        move.wait()
    push = thrusts(gathered(two) + missing[0], scale)
    step(two, one, push, 7, ROWS - 7, 2)
    push = thrusts(gathered(one) + missing[1], scale)
    step(one, two, push, 13, ROWS - 13, 3)

    stores = [pltpu.make_async_copy(two.at[pl.ds(H, NYD), c, pl.ds(0, NXD)], nest_out.at[c], out_sem.at[c]) for c in range(C)]
    for store in stores:
        store.start()

    def three(m):
        y = H + 3 * m
        return two[y] + two[y + 1] + two[y + 2]

    before, here = three(-1) * has_s, three(0)
    high_part, low_part = [], []
    for m in range(PYD):
        after = three(m + 1)
        if m == PYD - 1:
            after = after * has_n
        total = before + 2.0 * here + after
        part = pieces(total, 2)
        sum_v[C * m : C * m + C] = part[0]
        sum_v[C * (PYD + m) : C * (PYD + m) + C] = part[1]
        before, here = here, after
    mean = jnp.dot(sum_v[...], weight_in[...], preferred_element_type=F32)
    half = C * PYD
    for m in range(PYD):
        i = m + PH
        tiles = [new[i - 1, :, 128 * t : 128 * t + 128] + 2.0 * new[i, :, 128 * t : 128 * t + 128]
                 + new[i + 1, :, 128 * t : 128 * t + 128] for t in range(2)]
        from_w, from_e = shifted(tiles)
        direct = from_w[0] + 2.0 * tiles[0] + from_e[0]
        out_v[m] = direct * (1.0 / 32.0) + (mean[C * m : C * m + C] + mean[half + C * m : half + C * m + C]) * (1.0 / 288.0)
    last = [pltpu.make_async_copy(out_v.at[:, c, :], parent_out.at[c], out_sem.at[C + c]) for c in range(C)]
    for store in last:
        store.start()
    for store in stores + last:
        store.wait()


def solution(mesh):
    tiles_x, tiles_y = mesh.shape["gx"], mesh.shape["gy"]
    smem = pl.BlockSpec(memory_space=pltpu.SMEM)
    vmem = pl.BlockSpec(memory_space=pltpu.VMEM)
    anywhere = pl.BlockSpec(memory_space=pl.ANY)
    passed = ((NYD, C, NXD), (NEAR, C, NXD), (NEAR, C, NXD),
              (NYD // 16, C, 128), (NYD // 16, C, 128), (4, 2, C, 128), (2, C, 128), (9, C, 128),
              (ROWS, C, WIDE), (PROWS, C, PWIDE), (ROWS, C, 128), (ROWS, C, 128), (2, C, WIDE), (ROWS, 1, 256),
              (256, WIDE), (C, 128), (2, C, 128), (WIDE, 128))
    halved = (14, 17)

    def on_device(nest_wind, parent_wind, diffusion, drift, disk_sites, disk_live, disk_coef):
        rims = pl.pallas_call(
            functools.partial(exchange, tiles_x, tiles_y),
            out_shape=[pltpu.VMEM(shape, BF16 if i in halved else F32) for i, shape in enumerate(passed)],
            in_specs=[pl.BlockSpec(memory_space=pltpu.HBM)] * 7,
            out_specs=[vmem] * len(passed),
            scratch_shapes=[
                pltpu.VMEM((PYD, C, PXD), F32),
                pltpu.VMEM((PNEAR, C, PXD), F32),
                pltpu.VMEM((PNEAR, C, PXD), F32),
                pltpu.VMEM((PROWS, C, PWIDE), F32),
                pltpu.VMEM((NYD // 16, C, 128), F32),
                pltpu.VMEM((NYD // 16, C, 128), F32),
                pltpu.VMEM((4, C, 128), F32),
                pltpu.VMEM((4, C, 128), F32),
                pltpu.VMEM((2, C, 128), F32),
                pltpu.VMEM((4, C, 128), F32),
                pltpu.SMEM(diffusion.shape, F32),
                pltpu.SMEM(drift.shape, F32),
                pltpu.SMEM((2, 1, 1, MAXD), jnp.int32),
                pltpu.SMEM((1, 1, MAXD), jnp.int32),
                pltpu.SMEM((1, 1, MAXD), F32),
                pltpu.SemaphoreType.DMA((2 * C + 5,)),
                pltpu.SemaphoreType.DMA((20,)),
                pltpu.SemaphoreType.DMA((20,)),
            ],
            compiler_params=pltpu.CompilerParams(
                collective_id=0, has_side_effects=True, vmem_limit_bytes=16 * 2**20),
            name="exchange",
        )(*[pltpu.with_memory_space_constraint(x, pltpu.HBM) for x in
            (nest_wind, parent_wind, diffusion, drift, disk_sites, disk_live, disk_coef)])
        return tuple(pl.pallas_call(
            functools.partial(advance_all, tiles_x, tiles_y),
            out_shape=[jax.ShapeDtypeStruct(nest_wind.shape, F32), jax.ShapeDtypeStruct(parent_wind.shape, F32)],
            in_specs=[smem, smem] + [vmem] * len(passed),
            out_specs=[anywhere, anywhere],
            scratch_shapes=[
                pltpu.VMEM((ROWS, C, WIDE), F32),
                pltpu.VMEM((ROWS, C, WIDE), F32),
                pltpu.SMEM((9, 8, 128), F32),
                pltpu.VMEM((PYD, C, PXD), F32),
                pltpu.VMEM((2 * C * PYD, WIDE), BF16),
                pltpu.SemaphoreType.DMA((9,)),
                pltpu.SemaphoreType.DMA((2 * C,)),
            ],
            compiler_params=pltpu.CompilerParams(vmem_limit_bytes=40 * 2**20),
            name="advance",
        )(diffusion, drift, *rims))

    placed = (
        P(None, "gy", "gx"),
        P(None, "gy", "gx"),
        P(),
        P(),
        P(None, "gy", "gx", None),
        P("gy", "gx", None),
        P("gy", "gx", None),
    )
    return jax.shard_map(
        on_device,
        mesh=mesh,
        in_specs=placed,
        out_specs=(P(None, "gy", "gx"), P(None, "gy", "gx")),
        check_vma=False,
    )
```
